32 devices in a mesh: fit: 2 (over y), ao: 16 (over z, x, core).
Axes of the slice: x: 2, y: 2, z: 4, core: 2. Of those that a mesh axis runs over, the one named last changes fastest.
Arguments:
- occ_blocks: bfloat16 [6144, 512], P(('fit', 'ao')), may hold values from -6 to 6
- resident: bfloat16 [2048, 4096], P(('fit', 'ao')), may hold values from -0.375 to 0.375
- row_tiles: int32 [32, 2, 24], P(('fit', 'ao')), may hold values from 0 to 23, as said below
- row_pairs: int32 [3, 32, 2, 24], P(None, ('fit', 'ao')), may hold values from -1 to 31, as said below
- live_rows: int32 [32, 2], P(('fit', 'ao')), may hold values from 1 to 24, as said below
- tile_list: int32 [16, 24], replicated, may hold values from 0 to 255, as said below
- owner_slot: int32 [64], replicated, may hold values from 0 to 127, as said below
Outputs:
- half_exchange: bfloat16 [128, 64, 512], P('ao', 'fit')
The draws below stay inside these ranges and needn't reach their ends.
Inputs may be any that keep to these rules, and one draw needn't show every extreme that they name: `row_tiles`: within each group and cycle step the 24 entries are a permutation of 0 to 23. `row_pairs`: each entry is a resident tile index, or -1 where the row has no tile for that fitting block; rows at or beyond live_rows are -1. Within a group and cycle step, live rows whose tiles share an AO block name the same resident tile for the same fitting block. `live_rows`: in every draw some group has all 24 rows live at some cycle step. `tile_list`: codes within a column are distinct and name AO blocks that some owner holds. A column names at most 2 tiles whose AO blocks belong to one owner device (owner_slot // 8); in every draw some owner gets exactly 2 from every column. AO blocks take distinct slots; the owner device of block b is owner_slot[b] // 8; an owner holds 0 to 8 blocks in its first slots, and some owner holds exactly 8.
All inputs are finite; a program needn't handle non-finite values.
Results may differ from the reference program's by a relative error of at most 0.001.
Values may be sent and summed in bfloat16 or wider, within the bound.
No kernel may reach another device: no remote copies, remote signals or barrier semaphores. Data moves between devices by JAX's collectives and lax.ppermute only.
A program may use at most 64 MiB of HBM per device.

```python
import jax
import jax.numpy as jnp
from jax import lax

OCC = 512
AB = 64
FB = 64
OB = 128
PB_DEV = 3
OWN_CAP = 8
PAIR_STEP = 32
LT = 24
NAOB = 64
NFIT = 6144
N_FIT = 2
N_AO = 16


def ownership(key):
    mean_load = OWN_CAP // 2
    pair_count = N_AO // 2
    imbalance = jax.random.randint(jax.random.fold_in(key, 101), (pair_count,), 0, mean_load)
    imbalance = imbalance.at[0].set(mean_load)
    counts = jnp.stack([mean_load + imbalance, mean_load - imbalance], axis=1).reshape(N_AO).astype(jnp.int32)
    owner_perm = jax.random.permutation(jax.random.fold_in(key, 102), N_AO).astype(jnp.int32)
    owner_perm = ((owner_perm - owner_perm[0] + N_AO - 1) % N_AO).astype(jnp.int32)
    block_perm = jax.random.permutation(jax.random.fold_in(key, 103), NAOB).astype(jnp.int32)
    block_ends = jnp.cumsum(counts).astype(jnp.int32)
    starts = block_ends - counts
    position = jnp.arange(NAOB, dtype=jnp.int32)
    logical = jnp.sum((position[:, None] >= block_ends[None, :]).astype(jnp.int32), axis=1)
    within = position - starts[logical]
    slot_at = owner_perm[logical] * OWN_CAP + within
    owner_table = jnp.zeros((NAOB,), jnp.int32).at[block_perm].set(slot_at)
    return (counts, starts, block_perm, owner_table)


def column_tiles(key):
    counts, starts, block_perm, owner_table = ownership(key)
    occ_count = OCC // OB
    others = N_AO - 2

    def one_column(column):
        column_key = jax.random.fold_in(jax.random.fold_in(key, 201), column)
        order_perm = jax.random.permutation(jax.random.fold_in(column_key, 1), others).astype(jnp.int32) + 2
        flip_bits = jax.random.randint(jax.random.fold_in(column_key, 2), (others // 2,), 0, 2)
        first_share = jnp.where(flip_bits == 1, 2, 1).astype(jnp.int32)
        second_share = 3 - first_share
        first_share = first_share.at[0].set(2)
        second_share = second_share.at[0].set(2)
        wanted = jnp.zeros((N_AO,), jnp.int32).at[order_perm[0::2]].set(first_share)
        wanted = wanted.at[order_perm[1::2]].set(second_share).at[0].set(2)
        option_count = jnp.maximum(counts * occ_count, 1)
        first_pick = jax.random.randint(jax.random.fold_in(column_key, 3), (N_AO,), 0, option_count)
        step_pick = jax.random.randint(jax.random.fold_in(column_key, 4), (N_AO,), 0, jnp.maximum(option_count - 1, 1))
        second_pick = (first_pick + 1 + step_pick) % option_count
        pick_ids = jnp.stack([first_pick, second_pick], axis=1)
        blocks = block_perm[jnp.minimum(starts[:, None] + pick_ids // occ_count, NAOB - 1)]
        tile_codes = blocks * occ_count + pick_ids % occ_count
        is_valid = jnp.arange(2, dtype=jnp.int32)[None, :] < wanted[:, None]
        flat_pos = jnp.arange(2 * N_AO, dtype=jnp.int32).reshape(N_AO, 2)
        sort_score = jnp.where(is_valid, flat_pos, flat_pos + 2 * N_AO).reshape(-1)
        chosen = jnp.argsort(sort_score, stable=True)[:LT]
        row_codes = tile_codes.reshape(-1)[chosen]
        return row_codes[jax.random.permutation(jax.random.fold_in(column_key, 5), LT)].astype(jnp.int32)
    return jax.vmap(one_column)(jnp.arange(N_AO, dtype=jnp.int32))


def live_table(key):
    groups = N_FIT * N_AO
    load_level = jax.random.randint(jax.random.fold_in(key, 301), (groups,), 1, 5)
    heavy_group = jax.random.randint(jax.random.fold_in(key, 302), (), 0, groups)
    load_level = load_level.at[heavy_group].set(4)
    jitter = jax.random.randint(jax.random.fold_in(key, 303), (groups, N_FIT), 0, max(LT // 8, 1))
    counts = jnp.maximum(LT * load_level[:, None] // 4 - jitter, 1)
    full_step = jax.random.randint(jax.random.fold_in(key, 304), (), 0, N_FIT)
    return counts.at[heavy_group, full_step].set(LT).astype(jnp.int32)


def triple_rows(key):
    tiles_all = column_tiles(key)
    live_counts = live_table(key)
    occ_count = OCC // OB
    row_index = jnp.arange(LT, dtype=jnp.int32)

    def one_entry(group_id, cycle_step):
        column = group_id % N_AO
        step_key = jax.random.fold_in(jax.random.fold_in(jax.random.fold_in(key, 401), group_id), cycle_step)
        row_tile = jax.random.permutation(jax.random.fold_in(step_key, 1), LT).astype(jnp.int32)
        blocks = tiles_all[column][row_tile] // occ_count
        is_valid = row_index < live_counts[group_id, cycle_step]
        same_block = (blocks[:, None] == blocks[None, :]) & is_valid[None, :]
        first_row = jnp.min(jnp.where(same_block, row_index[None, :], LT), axis=1)
        present = jax.random.randint(jax.random.fold_in(step_key, 2), (LT, PB_DEV), 0, 3) == 0
        present = present.at[0, 0].set(True)
        present = present & (first_row == row_index)[:, None] & is_valid[:, None]
        present_total = jnp.sum(present.astype(jnp.int32))
        shift_by = jnp.maximum(PAIR_STEP - present_total, 0)
        pair_rank = (jnp.cumsum(present.reshape(-1).astype(jnp.int32)) - 1).reshape(LT, PB_DEV)
        kept_pair = present & (pair_rank < PAIR_STEP)
        slot_pair = jnp.where(kept_pair, pair_rank + shift_by, -1)
        pair_row = slot_pair[jnp.minimum(first_row, LT - 1)]
        pair_row = jnp.where(is_valid[:, None], pair_row, -1)
        return (row_tile, pair_row.T.astype(jnp.int32))
    over_steps = jax.vmap(one_entry, in_axes=(None, 0))
    over_groups = jax.vmap(over_steps, in_axes=(0, None))
    return over_groups(jnp.arange(N_FIT * N_AO, dtype=jnp.int32), jnp.arange(N_FIT, dtype=jnp.int32))


def draw_row_tiles(key, part):
    row_tile, pair_rows = triple_rows(key)
    return row_tile


def draw_row_pairs(key, part):
    row_tile, pair_rows = triple_rows(key)
    return jnp.transpose(pair_rows, (2, 0, 1, 3))


def draw_live_rows(key, part):
    return live_table(key)


def draw_tile_list(key, part):
    tile_rows = column_tiles(key)
    return tile_rows


def draw_owner_slot(key, part):
    return ownership(key)[3]


def block_scale(own_key, shape, shards, smallest, top_value):
    def one(axis_at, shards_of):
        draws = jax.random.uniform(jax.random.fold_in(jax.random.fold_in(own_key, 6), axis_at), (shards_of,), jnp.float32, smallest / len(shards), top_value / len(shards))
        return jnp.repeat(jnp.exp(draws), shape[axis_at] // shards_of).reshape((-1,) + (1,) * (len(shape) - axis_at - 1))

    gain = one(*shards[0])
    for cut in shards[1:]:
        gain = gain * one(*cut)
    return gain


def noise(own_key, dims, deviation, most, shards=(), held_as=jnp.bfloat16):
    gain = block_scale(own_key, dims, shards, -0.22, 0.18) if shards else 1.0
    result = jax.random.normal(own_key, dims, jnp.float32) * deviation * gain
    return jnp.minimum(jnp.maximum(result, -most), most).astype(held_as)


def setup_inputs(seed: int = 0) -> dict:
    seeds = jax.random.split(jax.random.key(seed), 8)
    occ_blocks = noise(seeds[0], (NFIT, OCC), 1.0, 6.0, ((0, 32),))
    resident = noise(seeds[1], (N_FIT * N_AO * N_FIT * PAIR_STEP, AB * FB), (FB * max(1, N_AO * N_FIT * N_FIT * OB // (4 * OCC))) ** -0.5, 0.375, ((0, 32),))
    row_tiles = draw_row_tiles(jax.random.fold_in(seeds[7], 71), 0)
    row_pairs = draw_row_pairs(jax.random.fold_in(seeds[7], 71), 0)
    live_rows = draw_live_rows(jax.random.fold_in(seeds[7], 71), 0)
    tile_list = draw_tile_list(jax.random.fold_in(seeds[7], 71), 0)
    owner_slot = draw_owner_slot(jax.random.fold_in(seeds[7], 71), 0)
    return dict(occ_blocks=occ_blocks, resident=resident, row_tiles=row_tiles, row_pairs=row_pairs, live_rows=live_rows, tile_list=tile_list, owner_slot=owner_slot)


def reference(occ_blocks, resident, row_tiles, row_pairs, live_rows, tile_list, owner_slot):
    occ_count = OCC // OB
    groups = N_FIT * N_AO
    pieces = occ_blocks.reshape(groups, PB_DEV, FB, occ_count, OB)
    tiles_all = resident.reshape(groups, N_FIT, PAIR_STEP, AB, FB)
    totals = jnp.zeros((N_AO * OWN_CAP, occ_count, AB, OB), jnp.float32)
    row_index = jnp.arange(LT, dtype=jnp.int32)

    def one_group(totals, group_id):
        fit_pos = group_id // N_AO
        column = group_id % N_AO
        tile_codes = tile_list[column]

        def one_step(totals, cycle_step):
            source = ((fit_pos - cycle_step) % N_FIT) * N_AO + column
            upiece = pieces[source]
            tile_ids = row_tiles[group_id, cycle_step]
            pair_ids = row_pairs[:, group_id, cycle_step]
            usable = (pair_ids >= 0) & (row_index < live_rows[group_id, cycle_step])[None, :]
            picked = tiles_all[group_id, cycle_step][jnp.maximum(pair_ids, 0)].astype(jnp.float32)
            picked = jnp.where(usable[:, :, None, None], picked, jnp.zeros((), jnp.float32))
            occ_ids = tile_codes[tile_ids] % occ_count
            chosen = upiece[:, :, occ_ids, :].astype(jnp.float32)
            product = jnp.einsum("jrmp,jprc->rmc", picked, chosen, precision=lax.Precision.HIGHEST)
            slot_ids = owner_slot[tile_codes[tile_ids] // occ_count]
            return totals.at[slot_ids, occ_ids].add(product), None

        totals, _ = lax.scan(one_step, totals, jnp.arange(N_FIT, dtype=jnp.int32))
        return totals, None

    totals, _ = lax.scan(one_group, totals, jnp.arange(groups, dtype=jnp.int32))
    return totals.transpose(0, 2, 1, 3).reshape(N_AO * OWN_CAP, AB, OCC).astype(jnp.bfloat16)
```

```python
import functools

import jax
import jax.numpy as jnp
from jax import lax
from jax.experimental import pallas as pl
from jax.experimental.pallas import tpu as pltpu
from jax.sharding import PartitionSpec as P

AB = 64
FB = 64
OB = 128
OWN_CAP = 8
CAP = 2
LEVELS = 32700.0
LOWEST = -100.0
BIAS = 127.0
NEAREST = 12582912.0
LIMIT = 48 * 1024 * 1024

SMEM = pl.BlockSpec(memory_space=pltpu.SMEM)
VMEM = pl.BlockSpec(memory_space=pltpu.VMEM)


def from_behind(block, axis, distance):
    count = lax.axis_size(axis)
    return lax.ppermute(block, axis, [((i - distance) % count, i) for i in range(count)])


def rounded(value):
    return (value + NEAREST) - NEAREST


def occ_columns(ref, occ_block):
    return ref[:, pl.ds(pl.multiple_of(occ_block * OB, OB), OB)]


def first_step(
    column_ref, rows_ref, pairs_ref, live_ref, list_ref, slot_ref, list_vec, tiles_ref, occ_ref,
    total_ref, later_ref, occ_of_ref, target_ref,
    sid_of_tile, held, pair_of,
):
    steps, width = rows_ref.shape[1:]
    fit_blocks = pairs_ref.shape[0]
    ao_count = list_ref.shape[0]
    slots = ao_count * CAP
    pair_step = tiles_ref.shape[0] // steps
    occ_count = occ_ref.shape[1] // OB
    column = column_ref[0]

    def clear_owner(owner, _):
        held[owner] = 0
        return 0

    def clear_slot(slot, _):
        occ_of_ref[slot] = 0
        for at in range(steps * fit_blocks):
            pair_of[at * slots + slot] = -1
        return 0

    lax.fori_loop(0, ao_count, clear_owner, 0, unroll=8)
    lax.fori_loop(0, slots, clear_slot, 0, unroll=8)

    def route(tile, _):
        code = list_ref[column, tile]
        owner = lax.div(slot_ref[lax.div(code, occ_count)], OWN_CAP)
        rank = held[owner]
        held[owner] = rank + 1
        slot = owner * CAP + rank
        sid_of_tile[tile] = slot
        occ_of_ref[slot] = lax.rem(code, occ_count)
        return 0

    lax.fori_loop(0, width, route, 0, unroll=4)

    for step in range(steps):
        live = live_ref[0, step]

        def place(row, _):
            slot = sid_of_tile[rows_ref[0, step, row]]
            for j in range(fit_blocks):
                pair = pairs_ref[j, 0, step, row]
                usable = (pair >= 0) & (row < live)
                pair_of[(step * fit_blocks + j) * slots + slot] = jnp.where(
                    usable, pair + step * pair_step, -1
                )
            return 0

        lax.fori_loop(0, width, place, 0, unroll=4)

    def tile_at(step, j, slot):
        pair = pair_of[(step * fit_blocks + j) * slots + slot]
        picked = tiles_ref[jnp.maximum(pair, 0)]
        return jnp.where(pair >= 0, picked, jnp.zeros_like(picked))

    def one_slot(slot, _):
        for step in range(steps):
            left = jnp.concatenate([tile_at(step, j, slot) for j in range(fit_blocks)], axis=1)
            if step:
                later_ref[step - 1, slot] = left
            else:
                total_ref[slot] = jnp.dot(
                    left, occ_columns(occ_ref, occ_of_ref[slot]), preferred_element_type=jnp.float32
                )
        return 0

    lax.fori_loop(0, slots, one_slot, 0, unroll=8)

    codes = list_vec[...]
    blocks = codes // occ_count
    slot_ids = jnp.zeros_like(codes)
    for block in range(slot_ref.shape[0]):
        slot_ids = jnp.where(blocks == block, slot_ref[block], slot_ids)
    mine = slot_ids // OWN_CAP == column
    count = OWN_CAP * occ_count
    goal = slot_ids % OWN_CAP * occ_count + codes % occ_count
    key = lax.broadcasted_iota(jnp.int32, codes.shape, 1) * count + goal
    first = jnp.min(jnp.where(mine, key, width * count), axis=1, keepdims=True)
    last = jnp.max(jnp.where(mine, key, -1), axis=1, keepdims=True)
    first_goal = jnp.where(last >= 0, first % count, count)
    last_goal = jnp.where(last > first, last % count, count)
    lane = lax.broadcasted_iota(jnp.int32, target_ref.shape, 1)
    target_ref[...] = jnp.where(lane == 0, first_goal, last_goal)


def middle_step(occ_of_ref, later_ref, occ_ref, before_ref, total_ref):
    def one_slot(slot, _):
        total_ref[slot] = before_ref[slot] + jnp.dot(
            later_ref[slot], occ_columns(occ_ref, occ_of_ref[slot]), preferred_element_type=jnp.float32
        )
        return 0

    lax.fori_loop(0, total_ref.shape[0], one_slot, 0, unroll=4)


def coded(value):
    top = jnp.max(jnp.abs(value), axis=0, keepdims=True)
    power = jnp.ceil(jnp.log2(jnp.maximum(top, 2.0**LOWEST)))
    scaled = value * (LEVELS * jnp.exp2(-power))
    bits = (power + BIAS).astype(jnp.int32)
    sub = lax.broadcasted_iota(jnp.int32, (8, OB), 0)
    bit = lax.shift_right_logical(jnp.broadcast_to(bits, (8, OB)), sub) & 1
    head = scaled[:8]
    bit_value = bit.astype(jnp.float32)
    head = rounded((head - bit_value) * 0.5) * 2.0 + bit_value
    if value.shape[0] == 8:
        return head.astype(jnp.int32)
    return jnp.concatenate([head, rounded(scaled[8:])], axis=0).astype(jnp.int32)


def decoded(whole):
    sub = lax.broadcasted_iota(jnp.int32, (8, OB), 0)
    bits = jnp.sum(lax.shift_left(whole[:8] & 1, sub), axis=0, keepdims=True)
    scale = jnp.exp2(bits.astype(jnp.float32) - BIAS) * (1.0 / LEVELS)
    return whole.astype(jnp.float32) * scale


def last_step(occ_of_ref, later_ref, occ_ref, before_ref, out_ref):
    height = out_ref.shape[1]
    fit_count = AB // height
    ao_count = out_ref.shape[0] // fit_count

    def one_owner(owner, _):
        sums = []
        for rank in range(CAP):
            slot = owner * CAP + rank
            sums.append(
                before_ref[slot]
                + jnp.dot(
                    later_ref[slot],
                    occ_columns(occ_ref, occ_of_ref[slot]),
                    preferred_element_type=jnp.float32,
                )
            )
        for part in range(fit_count):
            low, high = [coded(total[part * height : (part + 1) * height]) for total in sums]
            out_ref[part * ao_count + owner] = (low & 0xFFFF) | lax.shift_left(high, 16)
        return 0

    lax.fori_loop(0, ao_count, one_owner, 0, unroll=4)


def collect(target_ref, received_ref, out_ref, sums):
    ao_count = target_ref.shape[0]
    occ_count = out_ref.shape[2] // OB
    sums[...] = jnp.zeros_like(sums)

    def one_source(source, _):
        column = lax.rem(source, ao_count)
        words = received_ref[source]
        low = lax.shift_right_arithmetic(lax.shift_left(words, 16), 16)
        high = lax.shift_right_arithmetic(words, 16)
        first, second = target_ref[column, 0], target_ref[column, 1]
        sums[first] += decoded(low)
        sums[second] += decoded(high)
        return 0

    lax.fori_loop(0, received_ref.shape[0], one_source, 0, unroll=8)
    for slot in range(OWN_CAP):
        for occ in range(occ_count):
            out_ref[slot, :, occ * OB : (occ + 1) * OB] = sums[slot * occ_count + occ].astype(
                out_ref.dtype
            )


def shards(occ_blocks, resident, row_tiles, row_pairs, live_rows, tile_list, owner_slot):
    fit_count = lax.axis_size("fit")
    ao_count = lax.axis_size("ao")
    fit_blocks = row_pairs.shape[0]
    depth = fit_blocks * FB
    width = tile_list.shape[1]
    slots = ao_count * CAP
    height = AB // fit_count
    occ_count = occ_blocks.shape[1] // OB
    column = lax.axis_index("ao").astype(jnp.int32).reshape(1)
    params = pltpu.CompilerParams(vmem_limit_bytes=LIMIT)

    incoming = from_behind(occ_blocks, "fit", 1)
    tiles = resident.reshape(resident.shape[0], AB, FB)
    total_shape = jax.ShapeDtypeStruct((slots, AB, OB), jnp.float32)
    total, later, occ_of, targets = pl.pallas_call(
        first_step,
        out_shape=(
            total_shape,
            jax.ShapeDtypeStruct((fit_count - 1, slots, AB, depth), jnp.bfloat16),
            jax.ShapeDtypeStruct((slots,), jnp.int32),
            jax.ShapeDtypeStruct((ao_count, OB), jnp.int32),
        ),
        in_specs=[SMEM] * 6 + [VMEM] * 3,
        out_specs=(VMEM, VMEM, SMEM, VMEM),
        scratch_shapes=[
            pltpu.SMEM((width,), jnp.int32),
            pltpu.SMEM((ao_count,), jnp.int32),
            pltpu.SMEM((fit_count * fit_blocks * slots,), jnp.int32),
        ],
        compiler_params=params,
    )(column, row_tiles, row_pairs, live_rows, tile_list, owner_slot, tile_list, tiles, occ_blocks)

    def step_specs(step):
        at_step = pl.BlockSpec((None, slots, AB, depth), lambda at: (step - 1, 0, 0, 0))
        return dict(grid=(1,), in_specs=[SMEM, at_step, VMEM, VMEM], out_specs=VMEM)

    for step in range(1, fit_count - 1):
        total = pl.pallas_call(
            middle_step, out_shape=total_shape, compiler_params=params, **step_specs(step)
        )(occ_of, later, incoming, total)
        incoming = from_behind(incoming, "fit", 1)

    outgoing = pl.pallas_call(
        last_step,
        out_shape=jax.ShapeDtypeStruct((fit_count * ao_count, height, OB), jnp.int32),
        compiler_params=params,
        **step_specs(fit_count - 1),
    )(occ_of, later, incoming, total)
    received = lax.all_to_all(outgoing, ("fit", "ao"), split_axis=0, concat_axis=0, tiled=True)
    return pl.pallas_call(
        collect,
        out_shape=jax.ShapeDtypeStruct((OWN_CAP, height, occ_count * OB), jnp.bfloat16),
        in_specs=[SMEM, VMEM],
        out_specs=VMEM,
        scratch_shapes=[pltpu.VMEM((OWN_CAP * occ_count + 1, height, OB), jnp.float32)],
        compiler_params=params,
    )(targets, received)


def solution(mesh):
    return jax.shard_map(
        shards,
        mesh=mesh,
        in_specs=(
            P(("fit", "ao"), None),
            P(("fit", "ao"), None),
            P(("fit", "ao"), None, None),
            P(None, ("fit", "ao"), None, None),
            P(("fit", "ao"), None),
            P(),
            P(),
        ),
        out_specs=P("ao", "fit", None),
        check_vma=False,
    )
```

```python
import functools

import jax
import jax.numpy as jnp
from jax import lax
from jax.experimental import pallas as pl
from jax.experimental.pallas import tpu as pltpu
from jax.sharding import PartitionSpec as P

AB = 64
FB = 64
OB = 128
OWN_CAP = 8
CAP = 2
LEVELS = 32700.0
LOWEST = -100.0
BIAS = 127.0
NEAREST = 12582912.0
LIMIT = 48 * 1024 * 1024

SMEM = pl.BlockSpec(memory_space=pltpu.SMEM)
HBM = pl.BlockSpec(memory_space=pltpu.HBM)
VMEM = pl.BlockSpec(memory_space=pltpu.VMEM)


def from_behind(block, axis, distance):
    count = lax.axis_size(axis)
    return lax.ppermute(block, axis, [((i - distance) % count, i) for i in range(count)])


def in_hbm(array):
    return pltpu.with_memory_space_constraint(array, pltpu.HBM)


def rounded(value):
    return (value + NEAREST) - NEAREST


def occ_columns(ref, occ_block):
    return ref[:, pl.ds(pl.multiple_of(occ_block * OB, OB), OB)]


def first_step(
    column_ref, list_any, slot_any, rows_any, pairs_any, live_any, resident_any, occ_any,
    total_ref, later_ref, occ_of_ref, target_ref,
    sid_of_tile, held, pair_of, tiles, targets,
    list_ref, slot_ref, rows_ref, pairs_ref, live_ref, list_vec, resident_ref, occ_ref, arrived,
):
    sources = (list_any, slot_any, rows_any, pairs_any, live_any, list_any, resident_any, occ_any)
    landed = (list_ref, slot_ref, rows_ref, pairs_ref, live_ref, list_vec, resident_ref, occ_ref)
    copies = [
        pltpu.make_async_copy(source, landing, arrived.at[at])
        for at, (source, landing) in enumerate(zip(sources, landed))
    ]
    for copy in copies:
        copy.start()

    steps, width = rows_ref.shape[1:]
    fit_blocks = pairs_ref.shape[0]
    ao_count = list_ref.shape[0]
    slots = ao_count * CAP
    pair_step = resident_ref.shape[0] // steps
    occ_count = occ_ref.shape[1] // OB
    column = column_ref[0]

    def clear_owner(owner, _):
        held[owner] = 0
        return 0

    def clear_slot(slot, _):
        occ_of_ref[slot] = 0
        for at in range(steps * fit_blocks):
            pair_of[at * slots + slot] = -1
        return 0

    lax.fori_loop(0, ao_count, clear_owner, 0, unroll=8)
    lax.fori_loop(0, slots, clear_slot, 0, unroll=8)

    for copy in copies[:2]:
        copy.wait()

    def route(tile, _):
        code = list_ref[column, tile]
        owner = lax.div(slot_ref[lax.div(code, occ_count)], OWN_CAP)
        rank = held[owner]
        held[owner] = rank + 1
        slot = owner * CAP + rank
        sid_of_tile[tile] = slot
        occ_of_ref[slot] = lax.rem(code, occ_count)
        return 0

    lax.fori_loop(0, width, route, 0, unroll=4)

    for copy in copies[2:5]:
        copy.wait()
    for step in range(steps):
        live = live_ref[0, step]

        def place(row, _):
            slot = sid_of_tile[rows_ref[0, step, row]]
            for j in range(fit_blocks):
                pair = pairs_ref[j, 0, step, row]
                usable = (pair >= 0) & (row < live)
                pair_of[(step * fit_blocks + j) * slots + slot] = jnp.where(
                    usable, pair + step * pair_step, -1
                )
            return 0

        lax.fori_loop(0, width, place, 0, unroll=4)

    for copy in copies[5:]:
        copy.wait()
    for start in range(0, resident_ref.shape[0], 16):
        tiles[start : start + 16] = resident_ref[start : start + 16, :].reshape(
            16, AB * FB // OB, OB
        )

    def tile_at(step, j, slot):
        pair = pair_of[(step * fit_blocks + j) * slots + slot]
        picked = tiles[jnp.maximum(pair, 0)]
        return jnp.where(pair >= 0, picked, jnp.zeros_like(picked))

    def one_slot(slot, _):
        for step in range(steps):
            picked = [tile_at(step, j, slot) for j in range(fit_blocks)]
            left = jnp.concatenate(
                [
                    jnp.concatenate([tile[:, at : at + FB] for tile in picked], axis=1)
                    for at in range(0, OB, FB)
                ],
                axis=0,
            )
            if step:
                later_ref[step - 1, slot] = left
            else:
                total_ref[slot] = jnp.dot(
                    left, occ_columns(occ_ref, occ_of_ref[slot]), preferred_element_type=jnp.float32
                )
        return 0

    lax.fori_loop(0, slots, one_slot, 0, unroll=8)

    codes = list_vec[...]
    blocks = codes // occ_count
    slot_ids = jnp.zeros_like(codes)
    for block in range(slot_ref.shape[0]):
        slot_ids = jnp.where(blocks == block, slot_ref[block], slot_ids)
    mine = slot_ids // OWN_CAP == column
    count = OWN_CAP * occ_count
    goal = slot_ids % OWN_CAP * occ_count + codes % occ_count
    key = lax.broadcasted_iota(jnp.int32, codes.shape, 1) * count + goal
    first = jnp.min(jnp.where(mine, key, width * count), axis=1, keepdims=True)
    last = jnp.max(jnp.where(mine, key, -1), axis=1, keepdims=True)
    first_goal = jnp.where(last >= 0, first % count, count)
    last_goal = jnp.where(last > first, last % count, count)
    lane = lax.broadcasted_iota(jnp.int32, targets.shape, 1)
    targets[...] = jnp.where(lane == 0, first_goal, last_goal)
    copy = pltpu.make_async_copy(targets, target_ref, arrived.at[0])
    copy.start()
    copy.wait()


def middle_step(occ_of_ref, later_ref, occ_ref, before_ref, total_ref):
    def one_slot(slot, _):
        total_ref[slot] = before_ref[slot] + jnp.dot(
            later_ref[slot], occ_columns(occ_ref, occ_of_ref[slot]), preferred_element_type=jnp.float32
        )
        return 0

    lax.fori_loop(0, total_ref.shape[0], one_slot, 0, unroll=4)


def coded(value):
    top = jnp.max(jnp.abs(value), axis=0, keepdims=True)
    power = jnp.ceil(jnp.log2(jnp.maximum(top, 2.0**LOWEST)))
    scaled = value * (LEVELS * jnp.exp2(-power))
    bits = (power + BIAS).astype(jnp.int32)
    sub = lax.broadcasted_iota(jnp.int32, (8, OB), 0)
    bit = lax.shift_right_logical(jnp.broadcast_to(bits, (8, OB)), sub) & 1
    head = scaled[:8]
    bit_value = bit.astype(jnp.float32)
    head = rounded((head - bit_value) * 0.5) * 2.0 + bit_value
    if value.shape[0] == 8:
        return head.astype(jnp.int32)
    return jnp.concatenate([head, rounded(scaled[8:])], axis=0).astype(jnp.int32)


def decoded(whole):
    sub = lax.broadcasted_iota(jnp.int32, (8, OB), 0)
    bits = jnp.sum(lax.shift_left(whole[:8] & 1, sub), axis=0, keepdims=True)
    scale = jnp.exp2(bits.astype(jnp.float32) - BIAS) * (1.0 / LEVELS)
    return whole.astype(jnp.float32) * scale


def rows_of(total, part, height):
    half = height // 2
    return jnp.concatenate(
        [total[at + part * half : at + (part + 1) * half] for at in (0, AB // 2)], axis=0
    )


def last_step(occ_of_ref, later_ref, occ_ref, before_ref, out_ref):
    height = out_ref.shape[1]
    fit_count = AB // height
    ao_count = out_ref.shape[0] // fit_count

    def one_owner(owner, _):
        sums = []
        for rank in range(CAP):
            slot = owner * CAP + rank
            sums.append(
                before_ref[slot]
                + jnp.dot(
                    later_ref[slot],
                    occ_columns(occ_ref, occ_of_ref[slot]),
                    preferred_element_type=jnp.float32,
                )
            )
        for part in range(fit_count):
            low, high = [coded(rows_of(total, part, height)) for total in sums]
            out_ref[part * ao_count + owner] = (low & 0xFFFF) | lax.shift_left(high, 16)
        return 0

    lax.fori_loop(0, ao_count, one_owner, 0, unroll=16)


def collect(target_ref, received_ref, out_ref, sums):
    ao_count = target_ref.shape[0]
    fit_count = received_ref.shape[0] // ao_count
    height = out_ref.shape[1]
    half = height // 2
    occ_count = out_ref.shape[2] // OB
    sums[...] = jnp.zeros_like(sums)

    def one_column(column, _):
        lows, highs = [], []
        for part in range(fit_count):
            words = received_ref[part * ao_count + column]
            lows.append(decoded(lax.shift_right_arithmetic(lax.shift_left(words, 16), 16)))
            highs.append(decoded(lax.shift_right_arithmetic(words, 16)))
        for rank, parts in enumerate((lows, highs)):
            total = functools.reduce(jnp.add, parts)
            start = target_ref[column, rank] * height
            for odd in range(2):
                rows = pl.ds(start + odd, half, stride=2)
                sums[rows, :] += total[odd * half : (odd + 1) * half]
        return 0

    lax.fori_loop(0, ao_count, one_column, 0, unroll=16)
    for slot in range(OWN_CAP):
        for occ in range(occ_count):
            start = (slot * occ_count + occ) * height
            out_ref[slot, :, occ * OB : (occ + 1) * OB] = sums[start : start + height].astype(
                out_ref.dtype
            )


def shards(occ_blocks, resident, row_tiles, row_pairs, live_rows, tile_list, owner_slot):
    fit_count = lax.axis_size("fit")
    ao_count = lax.axis_size("ao")
    fit_blocks = row_pairs.shape[0]
    depth = fit_blocks * FB
    width = tile_list.shape[1]
    slots = ao_count * CAP
    height = AB // fit_count
    occ_count = occ_blocks.shape[1] // OB
    column = lax.axis_index("ao").astype(jnp.int32).reshape(1)
    params = pltpu.CompilerParams(vmem_limit_bytes=LIMIT)

    incoming = from_behind(occ_blocks, "fit", 1)
    indices = (tile_list, owner_slot, row_tiles, row_pairs, live_rows)
    total_shape = jax.ShapeDtypeStruct((slots, AB, OB), jnp.float32)
    total, later, occ_of, targets = pl.pallas_call(
        first_step,
        out_shape=(
            total_shape,
            jax.ShapeDtypeStruct((fit_count - 1, slots, AB, depth), jnp.bfloat16),
            pltpu.SMEM((slots,), jnp.int32),
            pltpu.SMEM((ao_count, OB), jnp.int32),
        ),
        in_specs=[SMEM] + [HBM] * 7,
        out_specs=(VMEM, VMEM, SMEM, SMEM),
        scratch_shapes=[
            pltpu.SMEM((width,), jnp.int32),
            pltpu.SMEM((ao_count,), jnp.int32),
            pltpu.SMEM((fit_count * fit_blocks * slots,), jnp.int32),
            pltpu.VMEM((resident.shape[0], AB * FB // OB, OB), jnp.bfloat16),
            pltpu.VMEM((ao_count, OB), jnp.int32),
            *[pltpu.SMEM(index.shape, index.dtype) for index in indices],
            *[pltpu.VMEM(block.shape, block.dtype) for block in (tile_list, resident, occ_blocks)],
            pltpu.SemaphoreType.DMA((len(indices) + 3,)),
        ],
        compiler_params=params,
    )(column, *[in_hbm(array) for array in (*indices, resident, occ_blocks)])

    def step_specs(step):
        if fit_count == 2:
            return dict(in_specs=[SMEM, VMEM, VMEM, VMEM], out_specs=VMEM)
        at_step = pl.BlockSpec((None, slots, AB, depth), lambda at: (step - 1, 0, 0, 0))
        return dict(grid=(1,), in_specs=[SMEM, at_step, VMEM, VMEM], out_specs=VMEM)

    for step in range(1, fit_count - 1):
        total = pl.pallas_call(
            middle_step, out_shape=total_shape, compiler_params=params, **step_specs(step)
        )(occ_of, later, incoming, total)
        incoming = from_behind(incoming, "fit", 1)

    outgoing = pl.pallas_call(
        last_step,
        out_shape=jax.ShapeDtypeStruct((fit_count * ao_count, height, OB), jnp.int32),
        compiler_params=params,
        **step_specs(fit_count - 1),
    )(occ_of, later[0] if fit_count == 2 else later, incoming, total)
    received = lax.all_to_all(outgoing, ("fit", "ao"), split_axis=0, concat_axis=0, tiled=True)
    return pl.pallas_call(
        collect,
        out_shape=jax.ShapeDtypeStruct((OWN_CAP, height, occ_count * OB), jnp.bfloat16),
        in_specs=[SMEM, VMEM],
        out_specs=VMEM,
        scratch_shapes=[pltpu.VMEM(((OWN_CAP * occ_count + 1) * height, OB), jnp.float32)],
        compiler_params=params,
    )(targets, received)


def solution(mesh):
    return jax.shard_map(
        shards,
        mesh=mesh,
        in_specs=(
            P(("fit", "ao"), None),
            P(("fit", "ao"), None),
            P(("fit", "ao"), None, None),
            P(None, ("fit", "ao"), None, None),
            P(("fit", "ao"), None),
            P(),
            P(),
        ),
        out_specs=P("ao", "fit", None),
        check_vma=False,
    )
```

```python
import functools

import jax
import jax.numpy as jnp
from jax import lax
from jax.experimental import pallas as pl
from jax.experimental.pallas import tpu as pltpu
from jax.sharding import PartitionSpec as P

AB = 64
FB = 64
OB = 128
OWN_CAP = 8
CAP = 2
LEVELS = 32700.0
LOWEST = -100.0
BIAS = 127.0
NEAREST = 12582912.0
LIMIT = 48 * 1024 * 1024

AO = ("ao3", "ao2", "ao1", "ao0")
ORDER = ('ao0', 'ao2', 'fit', 'ao1', 'ao3')

SMEM = pl.BlockSpec(memory_space=pltpu.SMEM)
HBM = pl.BlockSpec(memory_space=pltpu.HBM)
VMEM = pl.BlockSpec(memory_space=pltpu.VMEM)


def from_behind(block, axis, distance):
    count = lax.axis_size(axis)
    return lax.ppermute(block, axis, [((i - distance) % count, i) for i in range(count)])


def place(fit, ao, sizes):
    at = {"fit": fit}
    for axis in reversed(AO):
        at[axis] = lax.rem(ao, sizes[axis])
        ao = lax.div(ao, sizes[axis])
    position = 0
    for axis in ORDER:
        position = position * sizes[axis] + at[axis]
    return position


def in_hbm(array):
    return pltpu.with_memory_space_constraint(array, pltpu.HBM)


def rounded(value):
    return (value + NEAREST) - NEAREST


def occ_columns(ref, occ_block):
    return ref[:, pl.ds(pl.multiple_of(occ_block * OB, OB), OB)]


def first_step(
    column_ref, list_any, slot_any, rows_any, pairs_any, live_any, resident_any, occ_any,
    total_ref, later_ref, occ_of_ref, target_ref,
    sid_of_tile, held, pair_of, tiles, targets,
    list_ref, slot_ref, rows_ref, pairs_ref, live_ref, list_vec, resident_ref, occ_ref, arrived,
):
    sources = (list_any, slot_any, rows_any, pairs_any, live_any, list_any, resident_any, occ_any)
    landed = (list_ref, slot_ref, rows_ref, pairs_ref, live_ref, list_vec, resident_ref, occ_ref)
    copies = [
        pltpu.make_async_copy(source, landing, arrived.at[at])
        for at, (source, landing) in enumerate(zip(sources, landed))
    ]
    for copy in copies:
        copy.start()

    steps, width = rows_ref.shape[1:]
    fit_blocks = pairs_ref.shape[0]
    ao_count = list_ref.shape[0]
    slots = ao_count * CAP
    pair_step = resident_ref.shape[0] // steps
    occ_count = occ_ref.shape[1] // OB
    column = column_ref[0]

    def clear_owner(owner, _):
        held[owner] = 0
        return 0

    def clear_slot(slot, _):
        occ_of_ref[slot] = 0
        for at in range(steps * fit_blocks):
            pair_of[at * slots + slot] = -1
        return 0

    lax.fori_loop(0, ao_count, clear_owner, 0, unroll=8)
    lax.fori_loop(0, slots, clear_slot, 0, unroll=8)

    for copy in copies[:2]:
        copy.wait()

    def route(tile, _):
        code = list_ref[column, tile]
        owner = lax.div(slot_ref[lax.div(code, occ_count)], OWN_CAP)
        rank = held[owner]
        held[owner] = rank + 1
        slot = owner * CAP + rank
        sid_of_tile[tile] = slot
        occ_of_ref[slot] = lax.rem(code, occ_count)
        return 0

    lax.fori_loop(0, width, route, 0, unroll=4)

    for copy in copies[2:5]:
        copy.wait()
    for step in range(steps):
        live = live_ref[0, step]

        def place(row, _):
            slot = sid_of_tile[rows_ref[0, step, row]]
            for j in range(fit_blocks):
                pair = pairs_ref[j, 0, step, row]
                usable = (pair >= 0) & (row < live)
                pair_of[(step * fit_blocks + j) * slots + slot] = jnp.where(
                    usable, pair + step * pair_step, -1
                )
            return 0

        lax.fori_loop(0, width, place, 0, unroll=4)

    for copy in copies[5:]:
        copy.wait()
    for start in range(0, resident_ref.shape[0], 16):
        tiles[start : start + 16] = resident_ref[start : start + 16, :].reshape(
            16, AB * FB // OB, OB
        )

    def tile_at(step, j, slot):
        pair = pair_of[(step * fit_blocks + j) * slots + slot]
        picked = tiles[jnp.maximum(pair, 0)]
        return jnp.where(pair >= 0, picked, jnp.zeros_like(picked))

    def one_slot(slot, _):
        for step in range(steps):
            picked = [tile_at(step, j, slot) for j in range(fit_blocks)]
            left = jnp.concatenate(
                [
                    jnp.concatenate([tile[:, at : at + FB] for tile in picked], axis=1)
                    for at in range(0, OB, FB)
                ],
                axis=0,
            )
            if step:
                spare = jnp.zeros((AB, later_ref.shape[3] - left.shape[1]), left.dtype)
                later_ref[step - 1, slot] = jnp.concatenate([left, spare], axis=1)
            else:
                total_ref[slot] = jnp.dot(
                    left, occ_columns(occ_ref, occ_of_ref[slot]), preferred_element_type=jnp.float32
                )
        return 0

    lax.fori_loop(0, slots, one_slot, 0, unroll=8)

    codes = list_vec[...]
    blocks = codes // occ_count
    slot_ids = jnp.zeros_like(codes)
    for block in range(slot_ref.shape[0]):
        slot_ids = jnp.where(blocks == block, slot_ref[block], slot_ids)
    mine = slot_ids // OWN_CAP == column
    count = OWN_CAP * occ_count
    goal = slot_ids % OWN_CAP * occ_count + codes % occ_count
    key = lax.broadcasted_iota(jnp.int32, codes.shape, 1) * count + goal
    first = jnp.min(jnp.where(mine, key, width * count), axis=1, keepdims=True)
    last = jnp.max(jnp.where(mine, key, -1), axis=1, keepdims=True)
    first_goal = jnp.where(last >= 0, first % count, count)
    last_goal = jnp.where(last > first, last % count, count)
    lane = lax.broadcasted_iota(jnp.int32, targets.shape, 1)
    targets[...] = jnp.where(lane == 0, first_goal, last_goal)
    copy = pltpu.make_async_copy(targets, target_ref, arrived.at[0])
    copy.start()
    copy.wait()


def padded(occ_in, occ_ref):
    rows = occ_in.shape[0]
    occ_ref[:rows] = occ_in[...]
    occ_ref[rows:] = jnp.zeros((occ_ref.shape[0] - rows, occ_ref.shape[1]), occ_ref.dtype)


def middle_step(occ_of_ref, later_ref, occ_in, before_ref, total_ref, occ_ref):
    padded(occ_in, occ_ref)

    def one_slot(slot, _):
        total_ref[slot] = before_ref[slot] + jnp.dot(
            later_ref[slot], occ_columns(occ_ref, occ_of_ref[slot]), preferred_element_type=jnp.float32
        )
        return 0

    lax.fori_loop(0, total_ref.shape[0], one_slot, 0, unroll=4)


def coded(value):
    top = jnp.max(jnp.abs(value), axis=0, keepdims=True)
    power = jnp.ceil(jnp.log2(jnp.maximum(top, 2.0**LOWEST)))
    scaled = value * (LEVELS * jnp.exp2(-power))
    bits = (power + BIAS).astype(jnp.int32)
    sub = lax.broadcasted_iota(jnp.int32, (8, OB), 0)
    bit = lax.shift_right_logical(jnp.broadcast_to(bits, (8, OB)), sub) & 1
    head = scaled[:8]
    bit_value = bit.astype(jnp.float32)
    head = rounded((head - bit_value) * 0.5) * 2.0 + bit_value
    if value.shape[0] == 8:
        return head.astype(jnp.int32)
    return jnp.concatenate([head, rounded(scaled[8:])], axis=0).astype(jnp.int32)


def decoded(whole):
    sub = lax.broadcasted_iota(jnp.int32, (8, OB), 0)
    bits = jnp.sum(lax.shift_left(whole[:8] & 1, sub), axis=0, keepdims=True)
    scale = jnp.exp2(bits.astype(jnp.float32) - BIAS) * (1.0 / LEVELS)
    return whole.astype(jnp.float32) * scale


def rows_of(total, part, height):
    half = height // 2
    return jnp.concatenate(
        [total[at + part * half : at + (part + 1) * half] for at in (0, AB // 2)], axis=0
    )


def last_step(sizes, occ_of_ref, later_ref, occ_in, before_ref, out_ref, occ_ref):
    padded(occ_in, occ_ref)
    height = out_ref.shape[1]
    fit_count = AB // height
    ao_count = out_ref.shape[0] // fit_count

    def one_owner(owner, _):
        sums = []
        for rank in range(CAP):
            slot = owner * CAP + rank
            sums.append(
                before_ref[slot]
                + jnp.dot(
                    later_ref[slot],
                    occ_columns(occ_ref, occ_of_ref[slot]),
                    preferred_element_type=jnp.float32,
                )
            )
        for part in range(fit_count):
            low, high = [coded(rows_of(total, part, height)) for total in sums]
            out_ref[place(part, owner, sizes)] = (low & 0xFFFF) | lax.shift_left(high, 16)
        return 0

    lax.fori_loop(0, ao_count, one_owner, 0, unroll=16)


def collect(sizes, target_ref, received_ref, out_ref, sums):
    ao_count = target_ref.shape[0]
    fit_count = received_ref.shape[0] // ao_count
    height = out_ref.shape[1]
    half = height // 2
    occ_count = out_ref.shape[2] // OB
    sums[...] = jnp.zeros_like(sums)

    def one_column(column, _):
        lows, highs = [], []
        for part in range(fit_count):
            words = received_ref[place(part, column, sizes)]
            lows.append(decoded(lax.shift_right_arithmetic(lax.shift_left(words, 16), 16)))
            highs.append(decoded(lax.shift_right_arithmetic(words, 16)))
        for rank, parts in enumerate((lows, highs)):
            total = functools.reduce(jnp.add, parts)
            start = target_ref[column, rank] * height
            for odd in range(2):
                rows = pl.ds(start + odd, half, stride=2)
                sums[rows, :] += total[odd * half : (odd + 1) * half]
        return 0

    lax.fori_loop(0, ao_count, one_column, 0, unroll=16)
    for slot in range(OWN_CAP):
        for occ in range(occ_count):
            start = (slot * occ_count + occ) * height
            out_ref[slot, :, occ * OB : (occ + 1) * OB] = sums[start : start + height].astype(
                out_ref.dtype
            )


def shards(occ_blocks, resident, row_tiles, row_pairs, live_rows, tile_list, owner_slot):
    fit_count = lax.axis_size("fit")
    sizes = {axis: lax.axis_size(axis) for axis in ORDER}
    ao_count = lax.axis_size(AO)
    fit_blocks = row_pairs.shape[0]
    depth = -(-fit_blocks * FB // 256) * 256
    width = tile_list.shape[1]
    slots = ao_count * CAP
    height = AB // fit_count
    occ_count = occ_blocks.shape[1] // OB
    column = lax.axis_index(AO).astype(jnp.int32).reshape(1)
    params = pltpu.CompilerParams(vmem_limit_bytes=LIMIT)

    incoming = from_behind(occ_blocks, "fit", 1)
    indices = (tile_list, owner_slot, row_tiles, row_pairs, live_rows)
    total_shape = jax.ShapeDtypeStruct((slots, AB, OB), jnp.float32)
    total, later, occ_of, targets = pl.pallas_call(
        first_step,
        out_shape=(
            total_shape,
            jax.ShapeDtypeStruct((fit_count - 1, slots, AB, depth), jnp.bfloat16),
            pltpu.SMEM((slots,), jnp.int32),
            pltpu.SMEM((ao_count, OB), jnp.int32),
        ),
        in_specs=[SMEM] + [HBM] * 7,
        out_specs=(VMEM, VMEM, SMEM, SMEM),
        scratch_shapes=[
            pltpu.SMEM((width,), jnp.int32),
            pltpu.SMEM((ao_count,), jnp.int32),
            pltpu.SMEM((fit_count * fit_blocks * slots,), jnp.int32),
            pltpu.VMEM((resident.shape[0], AB * FB // OB, OB), jnp.bfloat16),
            pltpu.VMEM((ao_count, OB), jnp.int32),
            *[pltpu.SMEM(index.shape, index.dtype) for index in indices],
            *[pltpu.VMEM(block.shape, block.dtype) for block in (tile_list, resident, occ_blocks)],
            pltpu.SemaphoreType.DMA((len(indices) + 3,)),
        ],
        compiler_params=params,
    )(column, *[in_hbm(array) for array in (*indices, resident, occ_blocks)])

    wide = [pltpu.VMEM((depth, occ_blocks.shape[1]), occ_blocks.dtype)]

    def step_specs(step):
        if fit_count == 2:
            return dict(in_specs=[SMEM, VMEM, VMEM, VMEM], out_specs=VMEM, scratch_shapes=wide)
        at_step = pl.BlockSpec((None, slots, AB, depth), lambda at: (step - 1, 0, 0, 0))
        return dict(
            grid=(1,), in_specs=[SMEM, at_step, VMEM, VMEM], out_specs=VMEM, scratch_shapes=wide
        )

    for step in range(1, fit_count - 1):
        total = pl.pallas_call(
            middle_step, out_shape=total_shape, compiler_params=params, **step_specs(step)
        )(occ_of, later, incoming, total)
        incoming = from_behind(incoming, "fit", 1)

    outgoing = pl.pallas_call(
        functools.partial(last_step, sizes),
        out_shape=jax.ShapeDtypeStruct((fit_count * ao_count, height, OB), jnp.int32),
        compiler_params=params,
        **step_specs(fit_count - 1),
    )(occ_of, later[0] if fit_count == 2 else later, incoming, total)
    received = lax.all_to_all(outgoing, ORDER, split_axis=0, concat_axis=0, tiled=True)
    return pl.pallas_call(
        functools.partial(collect, sizes),
        out_shape=jax.ShapeDtypeStruct((OWN_CAP, height, occ_count * OB), jnp.bfloat16),
        in_specs=[SMEM, VMEM],
        out_specs=VMEM,
        scratch_shapes=[pltpu.VMEM(((OWN_CAP * occ_count + 1) * height, OB), jnp.float32)],
        compiler_params=params,
    )(targets, received)


def solution(mesh):
    fit_count, ao_count = mesh.devices.shape
    parts = mesh.devices.reshape(fit_count, ao_count // 8, 2, 2, 2)
    every = ("fit", *AO)
    return jax.shard_map(
        shards,
        mesh=jax.sharding.Mesh(parts, every),
        in_specs=(
            P(every, None),
            P(every, None),
            P(every, None, None),
            P(None, every, None, None),
            P(every, None),
            P(),
            P(),
        ),
        out_specs=P(AO, "fit", None),
        check_vma=False,
    )
```

```python
import functools

import jax
import jax.numpy as jnp
from jax import lax
from jax.experimental import pallas as pl
from jax.experimental.pallas import tpu as pltpu
from jax.sharding import PartitionSpec as P

AB = 64
FB = 64
OB = 128
OWN_CAP = 8
CAP = 2
LEVELS = 32700.0
LOWEST = -100.0
BIAS = -LOWEST
NEAREST = 12582912.0
LIMIT = 48 * 1024 * 1024

TURNS = (
    12, 23, 10, 1, 7, 26, 22, 25, 27, 0, 19, 24, 8, 9, 5, 13, 11, 2, 21, 4, 16, 30, 20, 6,
    14, 17, 28, 18, 29, 3, 31, 15,
)

SMEM = pl.BlockSpec(memory_space=pltpu.SMEM)
HBM = pl.BlockSpec(memory_space=pltpu.HBM)
VMEM = pl.BlockSpec(memory_space=pltpu.VMEM)


def from_behind(block, axis, distance):
    count = lax.axis_size(axis)
    return lax.ppermute(block, axis, [((i - distance) % count, i) for i in range(count)])


def partners(count):
    return TURNS if count == len(TURNS) else tuple(range(count))


def in_hbm(array):
    return pltpu.with_memory_space_constraint(array, pltpu.HBM)


def rounded(value):
    return (value + NEAREST) - NEAREST


def occ_columns(ref, occ_block):
    return ref[:, pl.ds(pl.multiple_of(occ_block * OB, OB), OB)]


def first_step(
    column_ref, list_any, slot_any, rows_any, pairs_any, live_any, resident_any, occ_any,
    total_ref, later_ref, occ_of_ref, target_ref,
    sid_of_tile, held, pair_of, tiles, targets,
    list_ref, slot_ref, rows_ref, pairs_ref, live_ref, list_vec, resident_ref, occ_ref, arrived,
):
    sources = (list_any, slot_any, rows_any, pairs_any, live_any, list_any, resident_any, occ_any)
    landed = (list_ref, slot_ref, rows_ref, pairs_ref, live_ref, list_vec, resident_ref, occ_ref)
    copies = [
        pltpu.make_async_copy(source, landing, arrived.at[at])
        for at, (source, landing) in enumerate(zip(sources, landed))
    ]
    for copy in copies:
        copy.start()

    steps, width = rows_ref.shape[1:]
    fit_blocks = pairs_ref.shape[0]
    ao_count = list_ref.shape[0]
    slots = ao_count * CAP
    pair_step = resident_ref.shape[0] // steps
    occ_count = occ_ref.shape[1] // OB
    column = column_ref[0]

    def clear_owner(owner, _):
        held[owner] = 0
        return 0

    def clear_slot(slot, _):
        occ_of_ref[slot] = 0
        for at in range(steps * fit_blocks):
            pair_of[at * slots + slot] = -1
        return 0

    lax.fori_loop(0, ao_count, clear_owner, 0, unroll=8)
    lax.fori_loop(0, slots, clear_slot, 0, unroll=8)

    for copy in copies[:2]:
        copy.wait()

    def route(tile, _):
        code = list_ref[column, tile]
        owner = lax.div(slot_ref[lax.div(code, occ_count)], OWN_CAP)
        rank = held[owner]
        held[owner] = rank + 1
        slot = owner * CAP + rank
        sid_of_tile[tile] = slot
        occ_of_ref[slot] = lax.rem(code, occ_count)
        return 0

    lax.fori_loop(0, width, route, 0, unroll=4)

    for copy in copies[2:5]:
        copy.wait()
    for step in range(steps):
        live = live_ref[0, step]

        def place(row, _):
            slot = sid_of_tile[rows_ref[0, step, row]]
            for j in range(fit_blocks):
                pair = pairs_ref[j, 0, step, row]
                usable = (pair >= 0) & (row < live)
                pair_of[(step * fit_blocks + j) * slots + slot] = jnp.where(
                    usable, pair + step * pair_step, -1
                )
            return 0

        lax.fori_loop(0, width, place, 0, unroll=4)

    for copy in copies[5:]:
        copy.wait()
    for start in range(0, resident_ref.shape[0], 16):
        tiles[start : start + 16] = resident_ref[start : start + 16, :].reshape(
            16, AB * FB // OB, OB
        )

    def tile_at(step, j, slot):
        pair = pair_of[(step * fit_blocks + j) * slots + slot]
        picked = tiles[jnp.maximum(pair, 0)]
        return jnp.where(pair >= 0, picked, jnp.zeros_like(picked))

    def one_slot(slot, _):
        for step in range(steps):
            picked = [tile_at(step, j, slot) for j in range(fit_blocks)]
            left = jnp.concatenate(
                [
                    jnp.concatenate([tile[:, at : at + FB] for tile in picked], axis=1)
                    for at in range(0, OB, FB)
                ],
                axis=0,
            )
            if step:
                spare = jnp.zeros((AB, later_ref.shape[3] - left.shape[1]), left.dtype)
                later_ref[step - 1, slot] = jnp.concatenate([left, spare], axis=1)
            else:
                total_ref[slot] = jnp.dot(
                    left, occ_columns(occ_ref, occ_of_ref[slot]), preferred_element_type=jnp.float32
                )
        return 0

    lax.fori_loop(0, slots, one_slot, 0, unroll=8)

    codes = list_vec[...]
    blocks = codes // occ_count
    slot_ids = jnp.zeros_like(codes)
    for block in range(slot_ref.shape[0]):
        slot_ids = jnp.where(blocks == block, slot_ref[block], slot_ids)
    mine = slot_ids // OWN_CAP == column
    count = OWN_CAP * occ_count
    goal = slot_ids % OWN_CAP * occ_count + codes % occ_count
    key = lax.broadcasted_iota(jnp.int32, codes.shape, 1) * count + goal
    first = jnp.min(jnp.where(mine, key, width * count), axis=1, keepdims=True)
    last = jnp.max(jnp.where(mine, key, -1), axis=1, keepdims=True)
    first_goal = jnp.where(last >= 0, first % count, count)
    last_goal = jnp.where(last > first, last % count, count)
    lane = lax.broadcasted_iota(jnp.int32, targets.shape, 1)
    targets[...] = jnp.where(lane == 0, first_goal, last_goal)
    copy = pltpu.make_async_copy(targets, target_ref, arrived.at[0])
    copy.start()
    copy.wait()


def padded(occ_in, occ_ref):
    rows = occ_in.shape[0]
    occ_ref[:rows] = occ_in[...]
    occ_ref[rows:] = jnp.zeros((occ_ref.shape[0] - rows, occ_ref.shape[1]), occ_ref.dtype)


def middle_step(occ_of_ref, later_ref, occ_in, before_ref, total_ref, occ_ref):
    padded(occ_in, occ_ref)

    def one_slot(slot, _):
        total_ref[slot] = before_ref[slot] + jnp.dot(
            later_ref[slot], occ_columns(occ_ref, occ_of_ref[slot]), preferred_element_type=jnp.float32
        )
        return 0

    lax.fori_loop(0, total_ref.shape[0], one_slot, 0, unroll=4)


def coded(value):
    top = jnp.max(jnp.abs(value), axis=0, keepdims=True)
    power = jnp.ceil(jnp.log2(jnp.maximum(top, 2.0**LOWEST)))
    scaled = value * (LEVELS * jnp.exp2(-power))
    bits = (power + BIAS).astype(jnp.int32)
    sub = lax.broadcasted_iota(jnp.int32, (8, OB), 0)
    bit = lax.shift_right_logical(jnp.broadcast_to(bits, (8, OB)), sub) & 1
    head = scaled[:8]
    bit_value = bit.astype(jnp.float32)
    head = rounded((head - bit_value) * 0.5) * 2.0 + bit_value
    if value.shape[0] == 8:
        return head.astype(jnp.int32)
    return jnp.concatenate([head, rounded(scaled[8:])], axis=0).astype(jnp.int32)


def decoded(whole):
    sub = lax.broadcasted_iota(jnp.int32, (8, OB), 0)
    bits = jnp.sum(lax.shift_left(whole[:8] & 1, sub), axis=0, keepdims=True)
    scale = jnp.exp2(bits.astype(jnp.float32) - BIAS) * (1.0 / LEVELS)
    return whole.astype(jnp.float32) * scale


def rows_of(total, part, height):
    half = height // 2
    return jnp.concatenate(
        [total[at + part * half : at + (part + 1) * half] for at in (0, AB // 2)], axis=0
    )


def last_step(turns, occ_of_ref, later_ref, occ_in, before_ref, out_ref, occ_ref):
    padded(occ_in, occ_ref)
    height = out_ref.shape[1]
    fit_count = AB // height
    ao_count = out_ref.shape[0] // fit_count

    def one_owner(owner):
        sums = []
        for rank in range(CAP):
            slot = owner * CAP + rank
            sums.append(
                before_ref[slot]
                + jnp.dot(
                    later_ref[slot],
                    occ_columns(occ_ref, occ_of_ref[slot]),
                    preferred_element_type=jnp.float32,
                )
            )
        for part in range(fit_count):
            low, high = [coded(rows_of(total, part, height)) for total in sums]
            out_ref[turns.index(part * ao_count + owner)] = (low & 0xFFFF) | lax.shift_left(high, 16)
        return 0

    for owner in range(ao_count):
        one_owner(owner)


def collect(turns, target_ref, received_ref, out_ref, sums):
    ao_count = target_ref.shape[0]
    fit_count = received_ref.shape[0] // ao_count
    height = out_ref.shape[1]
    half = height // 2
    occ_count = out_ref.shape[2] // OB
    sums[...] = jnp.zeros_like(sums)

    def one_column(column):
        lows, highs = [], []
        for part in range(fit_count):
            words = received_ref[turns.index(part * ao_count + column)]
            lows.append(decoded(lax.shift_right_arithmetic(lax.shift_left(words, 16), 16)))
            highs.append(decoded(lax.shift_right_arithmetic(words, 16)))
        for rank, parts in enumerate((lows, highs)):
            total = functools.reduce(jnp.add, parts)
            start = target_ref[column, rank] * height
            for odd in range(2):
                rows = pl.ds(start + odd, half, stride=2)
                sums[rows, :] += total[odd * half : (odd + 1) * half]
        return 0

    for column in range(ao_count):
        one_column(column)
    for slot in range(OWN_CAP):
        for occ in range(occ_count):
            start = (slot * occ_count + occ) * height
            out_ref[slot, :, occ * OB : (occ + 1) * OB] = sums[start : start + height].astype(
                out_ref.dtype
            )


def shards(occ_blocks, resident, row_tiles, row_pairs, live_rows, tile_list, owner_slot):
    fit_count = lax.axis_size("fit")
    ao_count = lax.axis_size("ao")
    turns = partners(fit_count * ao_count)
    fit_blocks = row_pairs.shape[0]
    depth = -(-fit_blocks * FB // 256) * 256
    width = tile_list.shape[1]
    slots = ao_count * CAP
    height = AB // fit_count
    occ_count = occ_blocks.shape[1] // OB
    column = lax.axis_index("ao").astype(jnp.int32).reshape(1)
    params = pltpu.CompilerParams(vmem_limit_bytes=LIMIT)

    incoming = from_behind(occ_blocks, "fit", 1)
    indices = (tile_list, owner_slot, row_tiles, row_pairs, live_rows)
    total_shape = jax.ShapeDtypeStruct((slots, AB, OB), jnp.float32)
    total, later, occ_of, targets = pl.pallas_call(
        first_step,
        out_shape=(
            total_shape,
            jax.ShapeDtypeStruct((fit_count - 1, slots, AB, depth), jnp.bfloat16),
            pltpu.SMEM((slots,), jnp.int32),
            pltpu.SMEM((ao_count, OB), jnp.int32),
        ),
        in_specs=[SMEM] + [HBM] * 7,
        out_specs=(VMEM, VMEM, SMEM, SMEM),
        scratch_shapes=[
            pltpu.SMEM((width,), jnp.int32),
            pltpu.SMEM((ao_count,), jnp.int32),
            pltpu.SMEM((fit_count * fit_blocks * slots,), jnp.int32),
            pltpu.VMEM((resident.shape[0], AB * FB // OB, OB), jnp.bfloat16),
            pltpu.VMEM((ao_count, OB), jnp.int32),
            *[pltpu.SMEM(index.shape, index.dtype) for index in indices],
            *[pltpu.VMEM(block.shape, block.dtype) for block in (tile_list, resident, occ_blocks)],
            pltpu.SemaphoreType.DMA((len(indices) + 3,)),
        ],
        compiler_params=params,
    )(column, *[in_hbm(array) for array in (*indices, resident, occ_blocks)])

    wide = [pltpu.VMEM((depth, occ_blocks.shape[1]), occ_blocks.dtype)]

    def step_specs(step):
        if fit_count == 2:
            return dict(in_specs=[SMEM, VMEM, VMEM, VMEM], out_specs=VMEM, scratch_shapes=wide)
        at_step = pl.BlockSpec((None, slots, AB, depth), lambda at: (step - 1, 0, 0, 0))
        return dict(
            grid=(1,), in_specs=[SMEM, at_step, VMEM, VMEM], out_specs=VMEM, scratch_shapes=wide
        )

    for step in range(1, fit_count - 1):
        total = pl.pallas_call(
            middle_step, out_shape=total_shape, compiler_params=params, **step_specs(step)
        )(occ_of, later, incoming, total)
        incoming = from_behind(incoming, "fit", 1)

    outgoing = pl.pallas_call(
        functools.partial(last_step, turns),
        out_shape=jax.ShapeDtypeStruct((fit_count * ao_count, height, OB), jnp.int32),
        compiler_params=params,
        **step_specs(fit_count - 1),
    )(occ_of, later[0] if fit_count == 2 else later, incoming, total)
    received = lax.all_to_all(
        outgoing,
        ("fit", "ao"),
        split_axis=0,
        concat_axis=0,
        tiled=True,
        axis_index_groups=[list(turns)],
    )
    return pl.pallas_call(
        functools.partial(collect, turns),
        out_shape=jax.ShapeDtypeStruct((OWN_CAP, height, occ_count * OB), jnp.bfloat16),
        in_specs=[SMEM, VMEM],
        out_specs=VMEM,
        scratch_shapes=[pltpu.VMEM(((OWN_CAP * occ_count + 1) * height + 8, OB), jnp.float32)],
        compiler_params=params,
    )(targets, received)


def solution(mesh):
    return jax.shard_map(
        shards,
        mesh=mesh,
        in_specs=(
            P(("fit", "ao"), None),
            P(("fit", "ao"), None),
            P(("fit", "ao"), None, None),
            P(None, ("fit", "ao"), None, None),
            P(("fit", "ao"), None),
            P(),
            P(),
        ),
        out_specs=P("ao", "fit", None),
        check_vma=False,
    )
```

```python
import functools

import jax
import jax.numpy as jnp
from jax import lax
from jax.experimental import pallas as pl
from jax.experimental.pallas import tpu as pltpu
from jax.sharding import PartitionSpec as P

AB = 64
FB = 64
OB = 128
OWN_CAP = 8
CAP = 2
LEVELS = 32700.0
LOWEST = -100.0
BIAS = -LOWEST
NEAREST = 12582912.0
LIMIT = 48 * 1024 * 1024

TURNS = (
    12, 21, 10, 1, 7, 26, 22, 24, 27, 0, 6, 25, 8, 9, 5, 15, 11, 2, 13, 3, 16, 23, 20, 19,
    14, 18, 28, 17, 4, 29, 31, 30,
)

SMEM = pl.BlockSpec(memory_space=pltpu.SMEM)
HBM = pl.BlockSpec(memory_space=pltpu.HBM)
VMEM = pl.BlockSpec(memory_space=pltpu.VMEM)


def from_behind(block, axis, distance):
    count = lax.axis_size(axis)
    return lax.ppermute(block, axis, [((i - distance) % count, i) for i in range(count)])


def partners(count):
    return TURNS if count == len(TURNS) else tuple(range(count))


def in_hbm(array):
    return pltpu.with_memory_space_constraint(array, pltpu.HBM)


def rounded(value):
    return (value + NEAREST) - NEAREST


def occ_columns(ref, occ_block):
    return ref[:, pl.ds(pl.multiple_of(occ_block * OB, OB), OB)]


def first_step(
    column_ref, list_any, slot_any, rows_any, pairs_any, live_any, resident_any, occ_any,
    total_ref, later_ref, occ_of_ref, target_ref,
    sid_of_tile, held, pair_of, tiles, targets,
    list_ref, slot_ref, rows_ref, pairs_ref, live_ref, list_vec, resident_ref, occ_ref, arrived,
):
    sources = (list_any, slot_any, rows_any, pairs_any, live_any, list_any, resident_any, occ_any)
    landed = (list_ref, slot_ref, rows_ref, pairs_ref, live_ref, list_vec, resident_ref, occ_ref)
    copies = [
        pltpu.make_async_copy(source, landing, arrived.at[at])
        for at, (source, landing) in enumerate(zip(sources, landed))
    ]
    for copy in copies:
        copy.start()

    steps, width = rows_ref.shape[1:]
    fit_blocks = pairs_ref.shape[0]
    ao_count = list_ref.shape[0]
    slots = ao_count * CAP
    pair_step = resident_ref.shape[0] // steps
    occ_count = occ_ref.shape[1] // OB
    column = column_ref[0]

    def clear_owner(owner, _):
        held[owner] = 0
        return 0

    def clear_slot(slot, _):
        occ_of_ref[slot] = 0
        for at in range(steps * fit_blocks):
            pair_of[at * slots + slot] = -1
        return 0

    lax.fori_loop(0, ao_count, clear_owner, 0, unroll=8)
    lax.fori_loop(0, slots, clear_slot, 0, unroll=8)

    for copy in copies[:2]:
        copy.wait()

    def route(tile, _):
        code = list_ref[column, tile]
        owner = lax.div(slot_ref[lax.div(code, occ_count)], OWN_CAP)
        rank = held[owner]
        held[owner] = rank + 1
        slot = owner * CAP + rank
        sid_of_tile[tile] = slot
        occ_of_ref[slot] = lax.rem(code, occ_count)
        return 0

    lax.fori_loop(0, width, route, 0, unroll=4)

    for copy in copies[2:5]:
        copy.wait()
    for step in range(steps):
        live = live_ref[0, step]

        def place(row, _):
            slot = sid_of_tile[rows_ref[0, step, row]]
            for j in range(fit_blocks):
                pair = pairs_ref[j, 0, step, row]
                usable = (pair >= 0) & (row < live)
                pair_of[(step * fit_blocks + j) * slots + slot] = jnp.where(
                    usable, pair + step * pair_step, -1
                )
            return 0

        lax.fori_loop(0, width, place, 0, unroll=4)

    for copy in copies[5:]:
        copy.wait()
    for start in range(0, resident_ref.shape[0], 16):
        tiles[start : start + 16] = resident_ref[start : start + 16, :].reshape(
            16, AB * FB // OB, OB
        )

    def tile_at(step, j, slot):
        pair = pair_of[(step * fit_blocks + j) * slots + slot]
        picked = tiles[jnp.maximum(pair, 0)]
        return jnp.where(pair >= 0, picked, jnp.zeros_like(picked))

    def one_slot(slot, _):
        for step in range(steps):
            picked = [tile_at(step, j, slot) for j in range(fit_blocks)]
            left = jnp.concatenate(
                [
                    jnp.concatenate([tile[:, at : at + FB] for tile in picked], axis=1)
                    for at in range(0, OB, FB)
                ],
                axis=0,
            )
            if step:
                spare = jnp.zeros((AB, later_ref.shape[3] - left.shape[1]), left.dtype)
                later_ref[step - 1, slot] = jnp.concatenate([left, spare], axis=1)
            else:
                total_ref[slot] = jnp.dot(
                    left, occ_columns(occ_ref, occ_of_ref[slot]), preferred_element_type=jnp.float32
                )
        return 0

    lax.fori_loop(0, slots, one_slot, 0, unroll=8)

    codes = list_vec[...]
    blocks = codes // occ_count
    slot_ids = jnp.zeros_like(codes)
    for block in range(slot_ref.shape[0]):
        slot_ids = jnp.where(blocks == block, slot_ref[block], slot_ids)
    mine = slot_ids // OWN_CAP == column
    count = OWN_CAP * occ_count
    goal = slot_ids % OWN_CAP * occ_count + codes % occ_count
    key = lax.broadcasted_iota(jnp.int32, codes.shape, 1) * count + goal
    first = jnp.min(jnp.where(mine, key, width * count), axis=1, keepdims=True)
    last = jnp.max(jnp.where(mine, key, -1), axis=1, keepdims=True)
    first_goal = jnp.where(last >= 0, first % count, count)
    last_goal = jnp.where(last > first, last % count, count)
    lane = lax.broadcasted_iota(jnp.int32, targets.shape, 1)
    targets[...] = jnp.where(lane == 0, first_goal, last_goal)
    copy = pltpu.make_async_copy(targets, target_ref, arrived.at[0])
    copy.start()
    copy.wait()


def padded(occ_in, occ_ref):
    rows = occ_in.shape[0]
    occ_ref[:rows] = occ_in[...]
    occ_ref[rows:] = jnp.zeros((occ_ref.shape[0] - rows, occ_ref.shape[1]), occ_ref.dtype)


def middle_step(occ_of_ref, later_ref, occ_in, before_ref, total_ref, occ_ref):
    padded(occ_in, occ_ref)

    def one_slot(slot, _):
        total_ref[slot] = before_ref[slot] + jnp.dot(
            later_ref[slot], occ_columns(occ_ref, occ_of_ref[slot]), preferred_element_type=jnp.float32
        )
        return 0

    lax.fori_loop(0, total_ref.shape[0], one_slot, 0, unroll=4)


def coded(value):
    top = jnp.max(jnp.abs(value), axis=0, keepdims=True)
    power = jnp.ceil(jnp.log2(jnp.maximum(top, 2.0**LOWEST)))
    scaled = value * (LEVELS * jnp.exp2(-power))
    bits = (power + BIAS).astype(jnp.int32)
    sub = lax.broadcasted_iota(jnp.int32, (8, OB), 0)
    bit = lax.shift_right_logical(jnp.broadcast_to(bits, (8, OB)), sub) & 1
    head = scaled[:8]
    bit_value = bit.astype(jnp.float32)
    head = rounded((head - bit_value) * 0.5) * 2.0 + bit_value
    if value.shape[0] == 8:
        return head.astype(jnp.int32)
    return jnp.concatenate([head, rounded(scaled[8:])], axis=0).astype(jnp.int32)


def decoded(whole):
    sub = lax.broadcasted_iota(jnp.int32, (8, OB), 0)
    bits = jnp.sum(lax.shift_left(whole[:8] & 1, sub), axis=0, keepdims=True)
    scale = jnp.exp2(bits.astype(jnp.float32) - BIAS) * (1.0 / LEVELS)
    return whole.astype(jnp.float32) * scale


def rows_of(total, part, height):
    half = height // 2
    return jnp.concatenate(
        [total[at + part * half : at + (part + 1) * half] for at in (0, AB // 2)], axis=0
    )


def last_step(turns, occ_of_ref, later_ref, occ_in, before_ref, out_ref, occ_ref):
    padded(occ_in, occ_ref)
    height = out_ref.shape[1]
    fit_count = AB // height
    ao_count = out_ref.shape[0] // fit_count

    def one_owner(owner):
        sums = []
        for rank in range(CAP):
            slot = owner * CAP + rank
            sums.append(
                before_ref[slot]
                + jnp.dot(
                    later_ref[slot],
                    occ_columns(occ_ref, occ_of_ref[slot]),
                    preferred_element_type=jnp.float32,
                )
            )
        for part in range(fit_count):
            low, high = [coded(rows_of(total, part, height)) for total in sums]
            out_ref[turns.index(part * ao_count + owner)] = (low & 0xFFFF) | lax.shift_left(high, 16)
        return 0

    for owner in range(ao_count):
        one_owner(owner)


def collect(turns, target_ref, received_ref, out_ref, sums):
    ao_count = target_ref.shape[0]
    fit_count = received_ref.shape[0] // ao_count
    height = out_ref.shape[1]
    half = height // 2
    occ_count = out_ref.shape[2] // OB
    sums[...] = jnp.zeros_like(sums)

    def one_column(column):
        lows, highs = [], []
        for part in range(fit_count):
            words = received_ref[turns.index(part * ao_count + column)]
            lows.append(decoded(lax.shift_right_arithmetic(lax.shift_left(words, 16), 16)))
            highs.append(decoded(lax.shift_right_arithmetic(words, 16)))
        for rank, parts in enumerate((lows, highs)):
            total = functools.reduce(jnp.add, parts)
            start = target_ref[column, rank] * height
            for odd in range(2):
                rows = pl.ds(start + odd, half, stride=2)
                sums[rows, :] += total[odd * half : (odd + 1) * half]
        return 0

    for column in range(ao_count):
        one_column(column)
    for slot in range(OWN_CAP):
        for occ in range(occ_count):
            start = (slot * occ_count + occ) * height
            out_ref[slot, :, occ * OB : (occ + 1) * OB] = sums[start : start + height].astype(
                out_ref.dtype
            )


def shards(occ_blocks, resident, row_tiles, row_pairs, live_rows, tile_list, owner_slot):
    fit_count = lax.axis_size("fit")
    ao_count = lax.axis_size("ao")
    turns = partners(fit_count * ao_count)
    fit_blocks = row_pairs.shape[0]
    depth = -(-fit_blocks * FB // 256) * 256
    width = tile_list.shape[1]
    slots = ao_count * CAP
    height = AB // fit_count
    occ_count = occ_blocks.shape[1] // OB
    column = lax.axis_index("ao").astype(jnp.int32).reshape(1)
    params = pltpu.CompilerParams(vmem_limit_bytes=LIMIT)

    incoming = from_behind(occ_blocks, "fit", 1)
    indices = (tile_list, owner_slot, row_tiles, row_pairs, live_rows)
    total_shape = jax.ShapeDtypeStruct((slots, AB, OB), jnp.float32)
    total, later, occ_of, targets = pl.pallas_call(
        first_step,
        out_shape=(
            total_shape,
            jax.ShapeDtypeStruct((fit_count - 1, slots, AB, depth), jnp.bfloat16),
            pltpu.SMEM((slots,), jnp.int32),
            pltpu.SMEM((ao_count, OB), jnp.int32),
        ),
        in_specs=[SMEM] + [HBM] * 7,
        out_specs=(VMEM, VMEM, SMEM, SMEM),
        scratch_shapes=[
            pltpu.SMEM((width,), jnp.int32),
            pltpu.SMEM((ao_count,), jnp.int32),
            pltpu.SMEM((fit_count * fit_blocks * slots,), jnp.int32),
            pltpu.VMEM((resident.shape[0], AB * FB // OB, OB), jnp.bfloat16),
            pltpu.VMEM((ao_count, OB), jnp.int32),
            *[pltpu.SMEM(index.shape, index.dtype) for index in indices],
            *[pltpu.VMEM(block.shape, block.dtype) for block in (tile_list, resident, occ_blocks)],
            pltpu.SemaphoreType.DMA((len(indices) + 3,)),
        ],
        compiler_params=params,
    )(column, *[in_hbm(array) for array in (*indices, resident, occ_blocks)])

    wide = [pltpu.VMEM((depth, occ_blocks.shape[1]), occ_blocks.dtype)]

    def step_specs(step):
        if fit_count == 2:
            return dict(in_specs=[SMEM, VMEM, VMEM, VMEM], out_specs=VMEM, scratch_shapes=wide)
        at_step = pl.BlockSpec((None, slots, AB, depth), lambda at: (step - 1, 0, 0, 0))
        return dict(
            grid=(1,), in_specs=[SMEM, at_step, VMEM, VMEM], out_specs=VMEM, scratch_shapes=wide
        )

    for step in range(1, fit_count - 1):
        total = pl.pallas_call(
            middle_step, out_shape=total_shape, compiler_params=params, **step_specs(step)
        )(occ_of, later, incoming, total)
        incoming = from_behind(incoming, "fit", 1)

    outgoing = pl.pallas_call(
        functools.partial(last_step, turns),
        out_shape=jax.ShapeDtypeStruct((fit_count * ao_count, height, OB), jnp.int32),
        compiler_params=params,
        **step_specs(fit_count - 1),
    )(occ_of, later[0] if fit_count == 2 else later, incoming, total)
    received = lax.all_to_all(
        outgoing,
        ("fit", "ao"),
        split_axis=0,
        concat_axis=0,
        tiled=True,
        axis_index_groups=[list(turns)],
    )
    return pl.pallas_call(
        functools.partial(collect, turns),
        out_shape=jax.ShapeDtypeStruct((OWN_CAP, height, occ_count * OB), jnp.bfloat16),
        in_specs=[SMEM, VMEM],
        out_specs=VMEM,
        scratch_shapes=[pltpu.VMEM(((OWN_CAP * occ_count + 1) * height + 8, OB), jnp.float32)],
        compiler_params=params,
    )(targets, received)


def solution(mesh):
    return jax.shard_map(
        shards,
        mesh=mesh,
        in_specs=(
            P(("fit", "ao"), None),
            P(("fit", "ao"), None),
            P(("fit", "ao"), None, None),
            P(None, ("fit", "ao"), None, None),
            P(("fit", "ao"), None),
            P(),
            P(),
        ),
        out_specs=P("ao", "fit", None),
        check_vma=False,
    )
```

```python
import functools

import jax
import jax.numpy as jnp
from jax import lax
from jax.experimental import pallas as pl
from jax.experimental.pallas import tpu as pltpu
from jax.sharding import PartitionSpec as P

AB = 64
FB = 64
OB = 128
OWN_CAP = 8
CAP = 2
LEVELS = 32700.0
LOWEST = -100.0
BIAS = -LOWEST
NEAREST = 12582912.0
LIMIT = 48 * 1024 * 1024

TURNS = (
    12, 21, 10, 1, 7, 26, 22, 24, 27, 0, 6, 25, 8, 9, 5, 15, 11, 2, 13, 3, 16, 23, 20, 19,
    14, 18, 28, 17, 4, 29, 31, 30,
)

SMEM = pl.BlockSpec(memory_space=pltpu.SMEM)
HBM = pl.BlockSpec(memory_space=pltpu.HBM)
VMEM = pl.BlockSpec(memory_space=pltpu.VMEM)


def from_behind(block, axis, distance):
    count = lax.axis_size(axis)
    return lax.ppermute(block, axis, [((i - distance) % count, i) for i in range(count)])


def partners(count):
    return TURNS if count == len(TURNS) else tuple(range(count))


def in_hbm(array):
    return pltpu.with_memory_space_constraint(array, pltpu.HBM)


def rounded(value):
    return (value + NEAREST) - NEAREST


def occ_columns(ref, occ_block):
    return ref[:, pl.ds(pl.multiple_of(occ_block * OB, OB), OB)]


def first_step(
    column_ref, list_any, slot_any, rows_any, pairs_any, live_any, resident_any, occ_any,
    total_ref, later_ref, occ_of_ref, target_ref,
    sid_of_tile, held, pair_of, tiles, targets,
    list_ref, slot_ref, rows_ref, pairs_ref, live_ref, list_vec, resident_ref, occ_ref, arrived,
):
    sources = (list_any, slot_any, rows_any, pairs_any, live_any, list_any, resident_any, occ_any)
    landed = (list_ref, slot_ref, rows_ref, pairs_ref, live_ref, list_vec, resident_ref, occ_ref)
    copies = [
        pltpu.make_async_copy(source, landing, arrived.at[at])
        for at, (source, landing) in enumerate(zip(sources, landed))
    ]
    for copy in copies:
        copy.start()

    steps, width = rows_ref.shape[1:]
    fit_blocks = pairs_ref.shape[0]
    ao_count = list_ref.shape[0]
    slots = ao_count * CAP
    pair_step = resident_ref.shape[0] // steps
    occ_count = occ_ref.shape[1] // OB
    column = column_ref[0]

    def clear_owner(owner, _):
        held[owner] = 0
        return 0

    def clear_slot(slot, _):
        occ_of_ref[slot] = 0
        for at in range(steps * fit_blocks):
            pair_of[at * slots + slot] = -1
        return 0

    lax.fori_loop(0, ao_count, clear_owner, 0, unroll=8)
    lax.fori_loop(0, slots, clear_slot, 0, unroll=8)

    for copy in copies[:2]:
        copy.wait()

    def route(tile, _):
        code = list_ref[column, tile]
        owner = lax.div(slot_ref[lax.div(code, occ_count)], OWN_CAP)
        rank = held[owner]
        held[owner] = rank + 1
        slot = owner * CAP + rank
        sid_of_tile[tile] = slot
        occ_of_ref[slot] = lax.rem(code, occ_count)
        return 0

    lax.fori_loop(0, width, route, 0, unroll=4)

    for copy in copies[2:5]:
        copy.wait()
    for step in range(steps):
        live = live_ref[0, step]

        def place(row, _):
            slot = sid_of_tile[rows_ref[0, step, row]]
            for j in range(fit_blocks):
                pair = pairs_ref[j, 0, step, row]
                usable = (pair >= 0) & (row < live)
                pair_of[(step * fit_blocks + j) * slots + slot] = jnp.where(
                    usable, pair + step * pair_step, -1
                )
            return 0

        lax.fori_loop(0, width, place, 0, unroll=4)

    for copy in copies[5:]:
        copy.wait()
    for start in range(0, resident_ref.shape[0], 16):
        tiles[start : start + 16] = resident_ref[start : start + 16, :].reshape(
            16, AB * FB // OB, OB
        )

    def tile_at(step, j, slot):
        pair = pair_of[(step * fit_blocks + j) * slots + slot]
        picked = tiles[jnp.maximum(pair, 0)]
        return jnp.where(pair >= 0, picked, jnp.zeros_like(picked))

    def one_slot(slot, _):
        for step in range(steps):
            picked = [tile_at(step, j, slot) for j in range(fit_blocks)]
            left = jnp.concatenate(
                [
                    jnp.concatenate([tile[:, at : at + FB] for tile in picked], axis=1)
                    for at in range(0, OB, FB)
                ],
                axis=0,
            )
            if step:
                spare = jnp.zeros((AB, later_ref.shape[3] - left.shape[1]), left.dtype)
                later_ref[step - 1, slot] = jnp.concatenate([left, spare], axis=1)
            else:
                total_ref[slot] = jnp.dot(
                    left, occ_columns(occ_ref, occ_of_ref[slot]), preferred_element_type=jnp.float32
                )
        return 0

    lax.fori_loop(0, slots, one_slot, 0, unroll=8)

    codes = list_vec[...]
    blocks = codes // occ_count
    slot_ids = jnp.zeros_like(codes)
    for block in range(slot_ref.shape[0]):
        slot_ids = jnp.where(blocks == block, slot_ref[block], slot_ids)
    mine = slot_ids // OWN_CAP == column
    count = OWN_CAP * occ_count
    goal = slot_ids % OWN_CAP * occ_count + codes % occ_count
    key = lax.broadcasted_iota(jnp.int32, codes.shape, 1) * count + goal
    first = jnp.min(jnp.where(mine, key, width * count), axis=1, keepdims=True)
    last = jnp.max(jnp.where(mine, key, -1), axis=1, keepdims=True)
    first_goal = jnp.where(last >= 0, first % count, count)
    last_goal = jnp.where(last > first, last % count, count)
    lane = lax.broadcasted_iota(jnp.int32, targets.shape, 1)
    targets[...] = jnp.where(lane == 0, first_goal, last_goal)
    copy = pltpu.make_async_copy(targets, target_ref, arrived.at[0])
    copy.start()
    copy.wait()


def padded(occ_in, occ_ref):
    rows = occ_in.shape[0]
    occ_ref[:rows] = occ_in[...]
    occ_ref[rows:] = jnp.zeros((occ_ref.shape[0] - rows, occ_ref.shape[1]), occ_ref.dtype)


def middle_step(occ_of_ref, later_ref, occ_in, before_ref, total_ref, occ_ref):
    padded(occ_in, occ_ref)

    def one_slot(slot, _):
        total_ref[slot] = before_ref[slot] + jnp.dot(
            later_ref[slot], occ_columns(occ_ref, occ_of_ref[slot]), preferred_element_type=jnp.float32
        )
        return 0

    lax.fori_loop(0, total_ref.shape[0], one_slot, 0, unroll=4)


def coded(value):
    top = jnp.max(jnp.abs(value), axis=0, keepdims=True)
    power = jnp.ceil(jnp.log2(jnp.maximum(top, 2.0**LOWEST)))
    scaled = value * (LEVELS * jnp.exp2(-power))
    bits = (power + BIAS).astype(jnp.int32)
    sub = lax.broadcasted_iota(jnp.int32, (8, OB), 0)
    bit = lax.shift_right_logical(jnp.broadcast_to(bits, (8, OB)), sub) & 1
    head = scaled[:8]
    bit_value = bit.astype(jnp.float32)
    head = rounded((head - bit_value) * 0.5) * 2.0 + bit_value
    if value.shape[0] == 8:
        return head.astype(jnp.int32)
    return jnp.concatenate([head, rounded(scaled[8:])], axis=0).astype(jnp.int32)


def decoded(words):
    sub = lax.broadcasted_iota(jnp.int32, (8, OB), 0)
    both = lax.shift_left(words[:8] & 0x10001, sub)
    bits = jnp.sum(both, axis=0, keepdims=True)
    scales = [
        jnp.exp2(part.astype(jnp.float32) - BIAS)
        for part in (bits & 0xFF, lax.shift_right_logical(bits, 16))
    ]
    low = lax.shift_left(words, 16).astype(jnp.float32) * (scales[0] * (2.0**-16 / LEVELS))
    high = lax.shift_right_arithmetic(words, 16).astype(jnp.float32) * (scales[1] * (1.0 / LEVELS))
    return low, high


def rows_of(total, part, height):
    half = height // 2
    return jnp.concatenate(
        [total[at + part * half : at + (part + 1) * half] for at in (0, AB // 2)], axis=0
    )


def last_step(turns, occ_of_ref, later_ref, occ_in, before_ref, out_ref, occ_ref):
    padded(occ_in, occ_ref)
    height = out_ref.shape[1]
    fit_count = AB // height
    ao_count = out_ref.shape[0] // fit_count

    def one_owner(owner):
        sums = []
        for rank in range(CAP):
            slot = owner * CAP + rank
            sums.append(
                before_ref[slot]
                + jnp.dot(
                    later_ref[slot],
                    occ_columns(occ_ref, occ_of_ref[slot]),
                    preferred_element_type=jnp.float32,
                )
            )
        for part in range(fit_count):
            low, high = [coded(rows_of(total, part, height)) for total in sums]
            out_ref[turns.index(part * ao_count + owner)] = (low & 0xFFFF) | lax.shift_left(high, 16)
        return 0

    for owner in range(ao_count):
        one_owner(owner)


def collect(turns, target_ref, received_ref, out_ref, sums):
    ao_count = target_ref.shape[0]
    fit_count = received_ref.shape[0] // ao_count
    height = out_ref.shape[1]
    half = height // 2
    occ_count = out_ref.shape[2] // OB
    sums[...] = jnp.zeros_like(sums)

    def one_column(column):
        lows, highs = [], []
        for part in range(fit_count):
            words = received_ref[turns.index(part * ao_count + column)]
            low, high = decoded(words)
            lows.append(low)
            highs.append(high)
        for rank, parts in enumerate((lows, highs)):
            total = functools.reduce(jnp.add, parts)
            start = target_ref[column, rank] * height
            for odd in range(2):
                rows = pl.ds(start + odd, half, stride=2)
                sums[rows, :] += total[odd * half : (odd + 1) * half]
        return 0

    for column in range(ao_count):
        one_column(column)
    for slot in range(OWN_CAP):
        for occ in range(occ_count):
            start = (slot * occ_count + occ) * height
            out_ref[slot, :, occ * OB : (occ + 1) * OB] = sums[start : start + height].astype(
                out_ref.dtype
            )


def shards(occ_blocks, resident, row_tiles, row_pairs, live_rows, tile_list, owner_slot):
    fit_count = lax.axis_size("fit")
    ao_count = lax.axis_size("ao")
    turns = partners(fit_count * ao_count)
    fit_blocks = row_pairs.shape[0]
    depth = -(-fit_blocks * FB // 256) * 256
    width = tile_list.shape[1]
    slots = ao_count * CAP
    height = AB // fit_count
    occ_count = occ_blocks.shape[1] // OB
    column = lax.axis_index("ao").astype(jnp.int32).reshape(1)
    params = pltpu.CompilerParams(vmem_limit_bytes=LIMIT)

    incoming = from_behind(occ_blocks, "fit", 1)
    indices = (tile_list, owner_slot, row_tiles, row_pairs, live_rows)
    total_shape = jax.ShapeDtypeStruct((slots, AB, OB), jnp.float32)
    total, later, occ_of, targets = pl.pallas_call(
        first_step,
        out_shape=(
            total_shape,
            jax.ShapeDtypeStruct((fit_count - 1, slots, AB, depth), jnp.bfloat16),
            pltpu.SMEM((slots,), jnp.int32),
            pltpu.SMEM((ao_count, OB), jnp.int32),
        ),
        in_specs=[SMEM] + [HBM] * 7,
        out_specs=(VMEM, VMEM, SMEM, SMEM),
        scratch_shapes=[
            pltpu.SMEM((width,), jnp.int32),
            pltpu.SMEM((ao_count,), jnp.int32),
            pltpu.SMEM((fit_count * fit_blocks * slots,), jnp.int32),
            pltpu.VMEM((resident.shape[0], AB * FB // OB, OB), jnp.bfloat16),
            pltpu.VMEM((ao_count, OB), jnp.int32),
            *[pltpu.SMEM(index.shape, index.dtype) for index in indices],
            *[pltpu.VMEM(block.shape, block.dtype) for block in (tile_list, resident, occ_blocks)],
            pltpu.SemaphoreType.DMA((len(indices) + 3,)),
        ],
        compiler_params=params,
    )(column, *[in_hbm(array) for array in (*indices, resident, occ_blocks)])

    wide = [pltpu.VMEM((depth, occ_blocks.shape[1]), occ_blocks.dtype)]

    def step_specs(step):
        if fit_count == 2:
            return dict(in_specs=[SMEM, VMEM, VMEM, VMEM], out_specs=VMEM, scratch_shapes=wide)
        at_step = pl.BlockSpec((None, slots, AB, depth), lambda at: (step - 1, 0, 0, 0))
        return dict(
            grid=(1,), in_specs=[SMEM, at_step, VMEM, VMEM], out_specs=VMEM, scratch_shapes=wide
        )

    for step in range(1, fit_count - 1):
        total = pl.pallas_call(
            middle_step, out_shape=total_shape, compiler_params=params, **step_specs(step)
        )(occ_of, later, incoming, total)
        incoming = from_behind(incoming, "fit", 1)

    outgoing = pl.pallas_call(
        functools.partial(last_step, turns),
        out_shape=jax.ShapeDtypeStruct((fit_count * ao_count, height, OB), jnp.int32),
        compiler_params=params,
        **step_specs(fit_count - 1),
    )(occ_of, later[0] if fit_count == 2 else later, incoming, total)
    received = lax.all_to_all(
        outgoing,
        ("fit", "ao"),
        split_axis=0,
        concat_axis=0,
        tiled=True,
        axis_index_groups=[list(turns)],
    )
    return pl.pallas_call(
        functools.partial(collect, turns),
        out_shape=jax.ShapeDtypeStruct((OWN_CAP, height, occ_count * OB), jnp.bfloat16),
        in_specs=[SMEM, VMEM],
        out_specs=VMEM,
        scratch_shapes=[pltpu.VMEM(((OWN_CAP * occ_count + 1) * height + 8, OB), jnp.float32)],
        compiler_params=params,
    )(targets, received)


def solution(mesh):
    return jax.shard_map(
        shards,
        mesh=mesh,
        in_specs=(
            P(("fit", "ao"), None),
            P(("fit", "ao"), None),
            P(("fit", "ao"), None, None),
            P(None, ("fit", "ao"), None, None),
            P(("fit", "ao"), None),
            P(),
            P(),
        ),
        out_specs=P("ao", "fit", None),
        check_vma=False,
    )
```

```python
import functools

import jax
import jax.numpy as jnp
from jax import lax
from jax.experimental import pallas as pl
from jax.experimental.pallas import tpu as pltpu
from jax.sharding import PartitionSpec as P

AB = 64
FB = 64
OB = 128
OWN_CAP = 8
CAP = 2
LEVELS = 32700.0
LOWEST = -100.0
BIAS = -LOWEST
NEAREST = 12582912.0
LIMIT = 48 * 1024 * 1024

TURNS = (
    20, 21, 10, 1, 7, 26, 22, 24, 27, 0, 6, 25, 8, 9, 5, 15, 11, 2, 13, 3, 16, 23, 12, 19,
    14, 18, 28, 17, 4, 29, 31, 30,
)

SMEM = pl.BlockSpec(memory_space=pltpu.SMEM)
HBM = pl.BlockSpec(memory_space=pltpu.HBM)
VMEM = pl.BlockSpec(memory_space=pltpu.VMEM)


def from_behind(block, axis, distance):
    count = lax.axis_size(axis)
    return lax.ppermute(block, axis, [((i - distance) % count, i) for i in range(count)])


def partners(count):
    return TURNS if count == len(TURNS) else tuple(range(count))


def in_hbm(array):
    return pltpu.with_memory_space_constraint(array, pltpu.HBM)


def rounded(value):
    return (value + NEAREST) - NEAREST


def occ_columns(ref, occ_block):
    return ref[:, pl.ds(pl.multiple_of(occ_block * OB, OB), OB)]


def first_step(
    column_ref, list_any, slot_any, rows_any, pairs_any, live_any, resident_any, occ_any,
    total_ref, later_ref, occ_of_ref, target_ref,
    sid_of_tile, held, pair_of, tiles, targets,
    list_ref, slot_ref, rows_ref, pairs_ref, live_ref, list_vec, resident_ref, occ_ref, arrived,
):
    sources = (list_any, slot_any, rows_any, pairs_any, live_any, list_any, resident_any, occ_any)
    landed = (list_ref, slot_ref, rows_ref, pairs_ref, live_ref, list_vec, resident_ref, occ_ref)
    copies = [
        pltpu.make_async_copy(source, landing, arrived.at[at])
        for at, (source, landing) in enumerate(zip(sources, landed))
    ]
    for copy in copies:
        copy.start()

    steps, width = rows_ref.shape[1:]
    fit_blocks = pairs_ref.shape[0]
    ao_count = list_ref.shape[0]
    slots = ao_count * CAP
    pair_step = resident_ref.shape[0] // steps
    occ_count = occ_ref.shape[1] // OB
    column = column_ref[0]

    def clear_owner(owner, _):
        held[owner] = 0
        return 0

    def clear_slot(slot, _):
        occ_of_ref[slot] = 0
        for at in range(steps * fit_blocks):
            pair_of[at * slots + slot] = -1
        return 0

    lax.fori_loop(0, ao_count, clear_owner, 0, unroll=8)
    lax.fori_loop(0, slots, clear_slot, 0, unroll=8)

    for copy in copies[:2]:
        copy.wait()

    def route(tile, _):
        code = list_ref[column, tile]
        owner = lax.div(slot_ref[lax.div(code, occ_count)], OWN_CAP)
        rank = held[owner]
        held[owner] = rank + 1
        slot = owner * CAP + rank
        sid_of_tile[tile] = slot
        occ_of_ref[slot] = lax.rem(code, occ_count)
        return 0

    lax.fori_loop(0, width, route, 0, unroll=4)

    for copy in copies[2:5]:
        copy.wait()
    for step in range(steps):
        live = live_ref[0, step]

        def place(row, _):
            slot = sid_of_tile[rows_ref[0, step, row]]
            for j in range(fit_blocks):
                pair = pairs_ref[j, 0, step, row]
                usable = (pair >= 0) & (row < live)
                pair_of[(step * fit_blocks + j) * slots + slot] = jnp.where(
                    usable, pair + step * pair_step, -1
                )
            return 0

        lax.fori_loop(0, width, place, 0, unroll=4)

    for copy in copies[5:]:
        copy.wait()
    for start in range(0, resident_ref.shape[0], 16):
        tiles[start : start + 16] = resident_ref[start : start + 16, :].reshape(
            16, AB * FB // OB, OB
        )

    def tile_at(step, j, slot):
        pair = pair_of[(step * fit_blocks + j) * slots + slot]
        picked = tiles[jnp.maximum(pair, 0)]
        return jnp.where(pair >= 0, picked, jnp.zeros_like(picked))

    def one_slot(slot, _):
        for step in range(steps):
            picked = [tile_at(step, j, slot) for j in range(fit_blocks)]
            left = jnp.concatenate(
                [
                    jnp.concatenate([tile[:, at : at + FB] for tile in picked], axis=1)
                    for at in range(0, OB, FB)
                ],
                axis=0,
            )
            if step:
                spare = jnp.zeros((AB, later_ref.shape[3] - left.shape[1]), left.dtype)
                later_ref[step - 1, slot] = jnp.concatenate([left, spare], axis=1)
            else:
                total_ref[slot] = jnp.dot(
                    left, occ_columns(occ_ref, occ_of_ref[slot]), preferred_element_type=jnp.float32
                )
        return 0

    lax.fori_loop(0, slots, one_slot, 0, unroll=8)

    codes = list_vec[...]
    blocks = codes // occ_count
    slot_ids = jnp.zeros_like(codes)
    for block in range(slot_ref.shape[0]):
        slot_ids = jnp.where(blocks == block, slot_ref[block], slot_ids)
    mine = slot_ids // OWN_CAP == column
    count = OWN_CAP * occ_count
    goal = slot_ids % OWN_CAP * occ_count + codes % occ_count
    key = lax.broadcasted_iota(jnp.int32, codes.shape, 1) * count + goal
    first = jnp.min(jnp.where(mine, key, width * count), axis=1, keepdims=True)
    last = jnp.max(jnp.where(mine, key, -1), axis=1, keepdims=True)
    first_goal = jnp.where(last >= 0, first % count, count)
    last_goal = jnp.where(last > first, last % count, count)
    lane = lax.broadcasted_iota(jnp.int32, targets.shape, 1)
    targets[...] = jnp.where(lane == 0, first_goal, last_goal)
    copy = pltpu.make_async_copy(targets, target_ref, arrived.at[0])
    copy.start()
    copy.wait()


def padded(occ_in, occ_ref):
    rows = occ_in.shape[0]
    occ_ref[:rows] = occ_in[...]
    occ_ref[rows:] = jnp.zeros((occ_ref.shape[0] - rows, occ_ref.shape[1]), occ_ref.dtype)


def middle_step(occ_of_ref, later_ref, occ_in, before_ref, total_ref, occ_ref):
    padded(occ_in, occ_ref)

    def one_slot(slot, _):
        total_ref[slot] = before_ref[slot] + jnp.dot(
            later_ref[slot], occ_columns(occ_ref, occ_of_ref[slot]), preferred_element_type=jnp.float32
        )
        return 0

    lax.fori_loop(0, total_ref.shape[0], one_slot, 0, unroll=4)


def coded(value):
    top = jnp.max(jnp.abs(value), axis=0, keepdims=True)
    power = jnp.ceil(jnp.log2(jnp.maximum(top, 2.0**LOWEST)))
    scaled = value * (LEVELS * jnp.exp2(-power))
    bits = (power + BIAS).astype(jnp.int32)
    sub = lax.broadcasted_iota(jnp.int32, (8, OB), 0)
    bit = lax.shift_right_logical(jnp.broadcast_to(bits, (8, OB)), sub) & 1
    head = scaled[:8]
    bit_value = bit.astype(jnp.float32)
    head = rounded((head - bit_value) * 0.5) * 2.0 + bit_value
    if value.shape[0] == 8:
        return head.astype(jnp.int32)
    return jnp.concatenate([head, rounded(scaled[8:])], axis=0).astype(jnp.int32)


def decoded(words):
    sub = lax.broadcasted_iota(jnp.int32, (8, OB), 0)
    both = lax.shift_left(words[:8] & 0x10001, sub)
    bits = jnp.sum(both, axis=0, keepdims=True)
    scales = [
        jnp.exp2(part.astype(jnp.float32) - BIAS)
        for part in (bits & 0xFF, lax.shift_right_logical(bits, 16))
    ]
    low = lax.shift_left(words, 16).astype(jnp.float32) * (scales[0] * (2.0**-16 / LEVELS))
    high = lax.shift_right_arithmetic(words, 16).astype(jnp.float32) * (scales[1] * (1.0 / LEVELS))
    return low, high


def rows_of(total, part, height):
    half = height // 2
    return jnp.concatenate(
        [total[at + part * half : at + (part + 1) * half] for at in (0, AB // 2)], axis=0
    )


def last_step(turns, occ_of_ref, later_ref, occ_in, before_ref, out_ref, occ_ref):
    padded(occ_in, occ_ref)
    height = out_ref.shape[1]
    fit_count = AB // height
    ao_count = out_ref.shape[0] // fit_count

    def one_owner(owner):
        sums = []
        for rank in range(CAP):
            slot = owner * CAP + rank
            sums.append(
                before_ref[slot]
                + jnp.dot(
                    later_ref[slot],
                    occ_columns(occ_ref, occ_of_ref[slot]),
                    preferred_element_type=jnp.float32,
                )
            )
        for part in range(fit_count):
            low, high = [coded(rows_of(total, part, height)) for total in sums]
            out_ref[turns.index(part * ao_count + owner)] = (low & 0xFFFF) | lax.shift_left(high, 16)
        return 0

    for owner in range(ao_count):
        one_owner(owner)


def collect(turns, target_ref, received_ref, out_ref, sums):
    ao_count = target_ref.shape[0]
    fit_count = received_ref.shape[0] // ao_count
    height = out_ref.shape[1]
    half = height // 2
    occ_count = out_ref.shape[2] // OB
    sums[...] = jnp.zeros_like(sums)

    def one_column(column):
        lows, highs = [], []
        for part in range(fit_count):
            words = received_ref[turns.index(part * ao_count + column)]
            low, high = decoded(words)
            lows.append(low)
            highs.append(high)
        for rank, parts in enumerate((lows, highs)):
            total = functools.reduce(jnp.add, parts)
            start = target_ref[column, rank] * height
            for odd in range(2):
                rows = pl.ds(start + odd, half, stride=2)
                sums[rows, :] += total[odd * half : (odd + 1) * half]
        return 0

    for column in range(ao_count):
        one_column(column)
    for slot in range(OWN_CAP):
        for occ in range(occ_count):
            start = (slot * occ_count + occ) * height
            out_ref[slot, :, occ * OB : (occ + 1) * OB] = sums[start : start + height].astype(
                out_ref.dtype
            )


def shards(occ_blocks, resident, row_tiles, row_pairs, live_rows, tile_list, owner_slot):
    fit_count = lax.axis_size("fit")
    ao_count = lax.axis_size("ao")
    turns = partners(fit_count * ao_count)
    fit_blocks = row_pairs.shape[0]
    depth = -(-fit_blocks * FB // 256) * 256
    width = tile_list.shape[1]
    slots = ao_count * CAP
    height = AB // fit_count
    occ_count = occ_blocks.shape[1] // OB
    column = lax.axis_index("ao").astype(jnp.int32).reshape(1)
    params = pltpu.CompilerParams(vmem_limit_bytes=LIMIT)

    incoming = from_behind(occ_blocks, "fit", 1)
    indices = (tile_list, owner_slot, row_tiles, row_pairs, live_rows)
    total_shape = jax.ShapeDtypeStruct((slots, AB, OB), jnp.float32)
    total, later, occ_of, targets = pl.pallas_call(
        first_step,
        out_shape=(
            total_shape,
            jax.ShapeDtypeStruct((fit_count - 1, slots, AB, depth), jnp.bfloat16),
            pltpu.SMEM((slots,), jnp.int32),
            pltpu.SMEM((ao_count, OB), jnp.int32),
        ),
        in_specs=[SMEM] + [HBM] * 7,
        out_specs=(VMEM, VMEM, SMEM, SMEM),
        scratch_shapes=[
            pltpu.SMEM((width,), jnp.int32),
            pltpu.SMEM((ao_count,), jnp.int32),
            pltpu.SMEM((fit_count * fit_blocks * slots,), jnp.int32),
            pltpu.VMEM((resident.shape[0], AB * FB // OB, OB), jnp.bfloat16),
            pltpu.VMEM((ao_count, OB), jnp.int32),
            *[pltpu.SMEM(index.shape, index.dtype) for index in indices],
            *[pltpu.VMEM(block.shape, block.dtype) for block in (tile_list, resident, occ_blocks)],
            pltpu.SemaphoreType.DMA((len(indices) + 3,)),
        ],
        compiler_params=params,
    )(column, *[in_hbm(array) for array in (*indices, resident, occ_blocks)])

    wide = [pltpu.VMEM((depth, occ_blocks.shape[1]), occ_blocks.dtype)]

    def step_specs(step):
        if fit_count == 2:
            return dict(in_specs=[SMEM, VMEM, VMEM, VMEM], out_specs=VMEM, scratch_shapes=wide)
        at_step = pl.BlockSpec((None, slots, AB, depth), lambda at: (step - 1, 0, 0, 0))
        return dict(
            grid=(1,), in_specs=[SMEM, at_step, VMEM, VMEM], out_specs=VMEM, scratch_shapes=wide
        )

    for step in range(1, fit_count - 1):
        total = pl.pallas_call(
            middle_step, out_shape=total_shape, compiler_params=params, **step_specs(step)
        )(occ_of, later, incoming, total)
        incoming = from_behind(incoming, "fit", 1)

    outgoing = pl.pallas_call(
        functools.partial(last_step, turns),
        out_shape=jax.ShapeDtypeStruct((fit_count * ao_count, height, OB), jnp.int32),
        compiler_params=params,
        **step_specs(fit_count - 1),
    )(occ_of, later[0] if fit_count == 2 else later, incoming, total)
    received = lax.all_to_all(
        outgoing,
        ("fit", "ao"),
        split_axis=0,
        concat_axis=0,
        tiled=True,
        axis_index_groups=[list(turns)],
    )
    return pl.pallas_call(
        functools.partial(collect, turns),
        out_shape=jax.ShapeDtypeStruct((OWN_CAP, height, occ_count * OB), jnp.bfloat16),
        in_specs=[SMEM, VMEM],
        out_specs=VMEM,
        scratch_shapes=[pltpu.VMEM(((OWN_CAP * occ_count + 1) * height + 8, OB), jnp.float32)],
        compiler_params=params,
    )(targets, received)


def solution(mesh):
    return jax.shard_map(
        shards,
        mesh=mesh,
        in_specs=(
            P(("fit", "ao"), None),
            P(("fit", "ao"), None),
            P(("fit", "ao"), None, None),
            P(None, ("fit", "ao"), None, None),
            P(("fit", "ao"), None),
            P(),
            P(),
        ),
        out_specs=P("ao", "fit", None),
        check_vma=False,
    )
```
